32 devices in a mesh: group: 4 (over y, core), member: 8 (over z, x).
Axes of the slice: x: 2, y: 2, z: 4, core: 2. Of those that a mesh axis runs over, the one named last changes fastest.
Arguments:
- volume_frac: float32 [256, 512, 256], P('group', 'member'), may hold values from 0 to 1
- velocity: bfloat16 [3, 256, 512, 256], P(None, 'group', 'member'), may hold values from -6 to 6
- drop_block: int32 [4, 8, 16], P('group', 'member'), may hold values from 0 to 255, as said below
- drop_owner: int32 [4, 8, 16, 1], P('group', 'member'), may hold values from 0 to 7; in each aligned block of 16 rows (0 to 15, 16 to 31, ..., all dimensions but the last counted through in order) at most 2 rows name the same one
- parcel_vel: float32 [4, 8, 8, 2, 3, 512], P('group', 'member'), may hold values from -6 to 6
- parcel_rate: float32 [4, 8, 8, 2, 512], P('group', 'member'), may hold values from 0.05 to 0.8
- parcel_weight: float32 [4, 8, 8, 2, 512], P('group', 'member'), may hold values from 0.3 to 3
- parcel_cell: int32 [4, 8, 8, 2, 512], P('group', 'member'), may hold values from 0 to 4095
Outputs:
- frac_next: float32 [256, 512, 256], P('group', 'member')
- velocity_next: bfloat16 [3, 256, 512, 256], P(None, 'group', 'member')
- parcel_next: float32 [4, 8, 8, 2, 3, 512], P('group', 'member')
The draws below stay inside these ranges and needn't reach their ends.
Inputs may be any that keep to these rules, and one draw needn't show every extreme that they name: `drop_block`: the 16 entries of one device are distinct. `drop_owner`: no owner gets more than 2 of one device's droplet blocks; some device sends exactly 2 to one owner.
All inputs are finite; a program needn't handle non-finite values.
Results may differ from the reference program's by a relative error of at most 0.001.
Values may be sent and summed in bfloat16 or wider, within the bound.
No kernel may reach another device: no remote copies, remote signals or barrier semaphores. Data moves between devices by JAX's collectives and lax.ppermute only.
A program may use at most 448 MiB of HBM per device.

```python
import math
import jax
import jax.numpy as jnp
import numpy as np
from jax import lax

CX = 64
CY = 64
CZ = 256
DROP_DEV = 16
CAP = 2
PT = 512
NB_DEV = 256
NX = 256
NY = 512
N_GROUP = 4
N_MEMBER = 8


def draw_drop_block(key, part):
    keys = jax.random.split(key, N_GROUP * N_MEMBER)
    chosen = jax.vmap(lambda one_key: jax.random.permutation(one_key, NB_DEV)[:DROP_DEV])(keys)
    return chosen.reshape(N_GROUP, N_MEMBER, DROP_DEV).astype(jnp.int32)


def with_ends(drawn, rng, least, largest):
    extent = drawn.shape
    spot = [jax.random.randint(jax.random.fold_in(rng, axis), (), 0, extent[axis]) for axis in range(len(extent))]
    drawn = drawn.at[tuple(spot)].set(least)
    longest = extent.index(max(extent))
    spot[longest] = (spot[longest] + 1) % extent[longest]
    return drawn.at[tuple(spot)].set(largest)


def level_of(stream_key, extent, cuts, low, largest):
    def one(position, parts):
        heights = jax.random.uniform(jax.random.fold_in(jax.random.fold_in(stream_key, 6), position), (parts,), jnp.float32, low / len(cuts), largest / len(cuts))
        return jnp.repeat(jnp.exp(heights), extent[position] // parts).reshape((-1,) + (1,) * (len(extent) - position - 1))

    loudness = one(*cuts[0])
    for cut in cuts[1:]:
        loudness = loudness * one(*cut)
    return loudness


def deal_out(stream_key, own, number, rows, amount, top, limit, lean):
    ranking = jax.random.permutation(stream_key, amount)
    heavy_load, usual = load_shares(amount, rows * top, limit, lean, True), load_shares(amount, rows * top, limit, lean, False)
    places = jnp.arange(amount)

    def named(sizes, rotation):
        used = int((sizes > 0).sum())
        fixed = max(1, used // 4)
        passed = fixed + (places - fixed + rotation * (used - fixed)) % max(1, amount - fixed)
        return jnp.zeros((amount,), jnp.int32).at[ranking[jnp.where(places < fixed, places, passed)]].set(jnp.asarray(sizes, jnp.int32))

    sizes = jnp.where(number % 4 == 0, named(heavy_load, number // 4), named(usual, number - number // 4 - 1))
    mixed = jax.random.permutation(jax.random.fold_in(own, 3), amount)
    donor, receiver = mixed[0:amount // 2 * 2:2], mixed[1:amount // 2 * 2:2]
    room = jnp.minimum(sizes[donor] - 1, limit - sizes[receiver]) // 2
    room = jnp.where((donor == ranking[0]) | (receiver == ranking[0]) | (sizes[receiver] == 0), 0, jnp.maximum(room, 0))
    passed = jax.random.randint(jax.random.fold_in(own, 4), (amount // 2,), 0, 1 << 20) % (room + 1)
    sizes = sizes.at[donor].add(-passed).at[receiver].add(passed)
    members = jnp.searchsorted(jnp.cumsum(sizes), jnp.arange(rows * top), side="right").astype(jnp.int32)
    table = members.reshape(top, rows).T
    table = table[jax.random.permutation(jax.random.fold_in(own, 1), rows)]
    rotation = jax.random.randint(jax.random.fold_in(own, 2), (rows, 1), 0, top)
    return jnp.take_along_axis(table, (jnp.arange(top)[None, :] + rotation) % top, axis=1)


def load_shares(amount, total, bound, lean, full):
    loads = [(1 << 20) // math.isqrt(standing ** lean) + 1 for standing in range(1, amount + 1)]
    largest = bound if full else min(bound, max(-(-total // amount), total * loads[0] // sum(loads)))
    least = 1 if total - largest >= amount - 1 else 0
    holding, rest = [largest] + [least] * (amount - 1), total - largest - least * (amount - 1)
    while rest > 0:
        movable = [i for i in range(1, amount) if holding[i] < largest] or [i for i in range(1, amount) if holding[i] < bound]
        mass, left = sum([loads[i] for i in movable]), rest
        for i in movable:
            addition = min(bound - holding[i], max(1, left * loads[i] // mass), rest)
            holding[i] = holding[i] + addition
            rest = rest - addition
    return np.array(holding)


def gaussian(key, extent, width, limit, shards=(), kind=jnp.bfloat16):
    result = width * jax.random.normal(key, extent, jnp.float32)
    if shards:
        result = result * level_of(key, extent, shards, -0.22, 0.18)
    return jnp.clip(result, -limit, limit).astype(kind)


def setup_inputs(seed: int = 0) -> dict:
    streams_of = jax.random.split(jax.random.key(seed), 9)
    volume_frac = jnp.clip(1.0 * jax.random.uniform(streams_of[0], (NX, NY, CZ), jnp.float32) ** level_of(streams_of[0], (NX, NY, CZ), ((0, 4), (1, 8)), -0.2, 0.2), 0.0, 1.0)
    velocity = gaussian(streams_of[1], (3, NX, NY, CZ), 1.0, 6.0, ((1, 4), (2, 8)))
    drop_block = draw_drop_block(jax.random.fold_in(streams_of[8], 71), 0)
    drop_owner_keys = jax.random.split(jax.random.fold_in(streams_of[3], 1), N_GROUP * N_MEMBER * DROP_DEV // DROP_DEV)
    drop_owner_turns = jax.random.permutation(jax.random.fold_in(streams_of[3], 3), N_GROUP * N_MEMBER * DROP_DEV // DROP_DEV)
    drop_owner = jax.vmap(lambda own, number: deal_out(jax.random.fold_in(streams_of[3], 2), own, number, DROP_DEV, N_MEMBER, 1, CAP, 2))(drop_owner_keys, drop_owner_turns).reshape((N_GROUP, N_MEMBER, DROP_DEV, 1))
    parcel_vel = gaussian(streams_of[4], (N_GROUP, N_MEMBER, N_MEMBER, CAP, 3, PT), 1.0, 6.0, ((0, 4), (1, 8)), jnp.float32)
    parcel_rate = jnp.clip(jnp.exp(math.log(0.8) - 2.7725887 * jax.random.uniform(streams_of[5], (N_GROUP, N_MEMBER, N_MEMBER, CAP, PT), jnp.float32) ** level_of(streams_of[5], (N_GROUP, N_MEMBER, N_MEMBER, CAP, PT), ((0, 4), (1, 8)), -0.2, 0.2)), 0.05, 0.8)
    parcel_weight = jnp.clip(jnp.exp(math.log(3.0) - 2.3025851 * jax.random.uniform(streams_of[6], (N_GROUP, N_MEMBER, N_MEMBER, CAP, PT), jnp.float32) ** level_of(streams_of[6], (N_GROUP, N_MEMBER, N_MEMBER, CAP, PT), ((0, 4), (1, 8)), -0.2, 0.2)), 0.3, 3.0)
    parcel_cell = with_ends(jax.random.randint(streams_of[7], (N_GROUP, N_MEMBER, N_MEMBER, CAP, PT), 0, 4096), jax.random.fold_in(streams_of[7], 1), 0, 4095).astype(jnp.int32)
    return {"volume_frac": volume_frac, "velocity": velocity, "drop_block": drop_block, "drop_owner": drop_owner, "parcel_vel": parcel_vel, "parcel_rate": parcel_rate, "parcel_weight": parcel_weight, "parcel_cell": parcel_cell}


courant = 0.025


def face_div(frac_pad, speed_pad, along):
    inner = [slice(1, -1)] * 3
    lower_cut = list(inner)
    lower_cut[along] = slice(0, -1)
    upper_cut = list(inner)
    upper_cut[along] = slice(1, None)
    left_frac = frac_pad[tuple(lower_cut)]
    right_frac = frac_pad[tuple(upper_cut)]
    left_speed = speed_pad[tuple(lower_cut)]
    face_flux = courant * (jnp.maximum(left_speed, 0.0) * left_frac + jnp.minimum(left_speed, 0.0) * right_frac)
    length = face_flux.shape[along]
    return lax.slice_in_dim(face_flux, 1, length, axis=along) - lax.slice_in_dim(face_flux, 0, length - 1, axis=along)


def drag_one(block_data, parcel_v, drag_rate, weight, cell_ids):
    sampled = block_data[:, cell_ids].astype(jnp.float32)
    gas_share = 1.0 - sampled[3]
    acceleration = drag_rate * gas_share * (sampled[:3] - parcel_v)
    deposit_w = (weight * acceleration).astype(jnp.bfloat16)
    source = jnp.zeros((3, 4096), jnp.float32).at[:, cell_ids].add(deposit_w.astype(jnp.float32))
    return parcel_v + acceleration, source.astype(jnp.bfloat16)


def reference(volume_frac, velocity, drop_block, drop_owner, parcel_vel, parcel_rate, parcel_weight, parcel_cell):
    frac_pad = jnp.pad(volume_frac, 1)
    speed_pad = jnp.pad(velocity.astype(jnp.float32), ((0, 0), (1, 1), (1, 1), (1, 1)))
    change = face_div(frac_pad, speed_pad[0], 0) + face_div(frac_pad, speed_pad[1], 1) + face_div(frac_pad, speed_pad[2], 2)
    frac_next = jnp.minimum(volume_frac - change, 1.0)
    owners = drop_owner[..., 0]
    positions = jnp.arange(DROP_DEV, dtype=jnp.int32)
    earlier = positions[:, None] < positions[None, :]
    places = jnp.sum(((owners[..., :, None] == owners[..., None, :]) & earlier).astype(jnp.int32), axis=-2).astype(jnp.int32)

    def per_group(group_idx):
        frac_slab = lax.dynamic_slice_in_dim(volume_frac, group_idx * CX, CX, 0)
        vel_slab = lax.dynamic_slice_in_dim(velocity, group_idx * CX, CX, 1)
        combined = jnp.concatenate([vel_slab, frac_slab[None].astype(jnp.bfloat16)], 0)
        blocks = combined.reshape(4, CX // 16, 16, N_MEMBER, CY // 16, 16, CZ // 16, 16)
        blocks = blocks.transpose(3, 1, 4, 6, 0, 2, 5, 7).reshape(N_MEMBER, NB_DEV, 4, 4096)
        block_ids = drop_block[group_idx]
        picked = jnp.take_along_axis(blocks, block_ids[:, :, None, None], axis=1)
        owner_row = owners[group_idx]
        place_row = places[group_idx]
        source_row = jnp.broadcast_to(jnp.arange(N_MEMBER, dtype=jnp.int32)[:, None], owner_row.shape)
        got_vel = parcel_vel[group_idx][owner_row, source_row, place_row]
        got_rate = parcel_rate[group_idx][owner_row, source_row, place_row]
        got_weight = parcel_weight[group_idx][owner_row, source_row, place_row]
        got_cell = parcel_cell[group_idx][owner_row, source_row, place_row]
        new_vel, source = jax.vmap(jax.vmap(drag_one))(picked, got_vel, got_rate, got_weight, got_cell)
        vel_out = parcel_vel[group_idx].at[owner_row, source_row, place_row].set(new_vel)
        deposit = jnp.zeros((N_MEMBER, NB_DEV, 3, 4096), jnp.float32).at[source_row, block_ids].add(source.astype(jnp.float32))
        deposit = deposit.reshape(N_MEMBER, CX // 16, CY // 16, CZ // 16, 3, 16, 16, 16)
        drag_field = deposit.transpose(4, 1, 5, 0, 2, 6, 3, 7).reshape(3, CX, NY, CZ)
        return vel_out, drag_field

    parcel_next, drag_field = lax.map(per_group, jnp.arange(N_GROUP, dtype=jnp.int32))
    drag_field = drag_field.transpose(1, 0, 2, 3, 4).reshape(3, NX, NY, CZ)
    velocity_next = (velocity.astype(jnp.float32) + drag_field).astype(jnp.bfloat16)
    return (frac_next, velocity_next, parcel_next)
```

```python
import functools

import jax
import jax.numpy as jnp
from jax import lax
from jax.experimental import pallas as pl
from jax.experimental.pallas import tpu as pltpu
from jax.sharding import PartitionSpec as P

CAP = 2
EDGE = 16
LANES = 128
FIELDS = 6

courant = 0.025

F32 = jnp.float32
BF16 = jnp.bfloat16


def passed_along(block, axis, distance):
    devices = range(lax.axis_size(axis))
    route = [(i - distance, i) for i in devices if i - distance in devices]
    return lax.ppermute(block, axis, route)


def whole(shape):
    return pl.BlockSpec(shape, lambda *_: (0,) * len(shape))


def params(**more):
    return pltpu.CompilerParams(vmem_limit_bytes=56 * 1024 * 1024, **more)


def pack_body(
    vel_ref, rate_ref, weight_ref, cell_ref,
    f_first_x, f_last_x, u_last_x, f_first_y, f_last_y, u_last_y,
    parcels_ref, up_x, down_x, up_y, down_y,
):
    parcels_ref[:, 0:3] = vel_ref[...]
    parcels_ref[:, 3] = rate_ref[...]
    parcels_ref[:, 4] = weight_ref[...]
    parcels_ref[:, 5] = cell_ref[...].astype(F32)
    up_x[0] = f_last_x[0].astype(BF16)
    up_x[1] = u_last_x[0, 0]
    down_x[0] = f_first_x[0].astype(BF16)
    up_y[0] = f_last_y[:, 7, :].astype(BF16)
    up_y[1] = u_last_y[0].astype(F32)[:, 15, :].astype(BF16)
    down_y[0] = f_first_y[:, 0, :].astype(BF16)


def pack(volume_frac, velocity, vel, rate, weight, cell):
    nx, ny, nz = volume_frac.shape
    members, _, parcels = rate.shape
    return pl.pallas_call(
        pack_body,
        grid=(1,),
        in_specs=[
            whole(vel.shape),
            whole(rate.shape),
            whole(weight.shape),
            whole(cell.shape),
            pl.BlockSpec((1, ny, nz), lambda i: (0, 0, 0)),
            pl.BlockSpec((1, ny, nz), lambda i: (nx - 1, 0, 0)),
            pl.BlockSpec((1, 1, ny, nz), lambda i: (0, nx - 1, 0, 0)),
            pl.BlockSpec((nx, 8, nz), lambda i: (0, 0, 0)),
            pl.BlockSpec((nx, 8, nz), lambda i: (0, ny // 8 - 1, 0)),
            pl.BlockSpec((1, nx, 16, nz), lambda i: (1, 0, ny // 16 - 1, 0)),
        ],
        out_specs=[
            whole((members, FIELDS, CAP, parcels)),
            whole((2, ny, nz)),
            whole((1, ny, nz)),
            whole((2, nx, nz)),
            whole((1, nx, nz)),
        ],
        out_shape=[
            jax.ShapeDtypeStruct((members, FIELDS, CAP, parcels), F32),
            jax.ShapeDtypeStruct((2, ny, nz), BF16),
            jax.ShapeDtypeStruct((1, ny, nz), BF16),
            jax.ShapeDtypeStruct((2, nx, nz), BF16),
            jax.ShapeDtypeStruct((1, nx, nz), BF16),
        ],
        compiler_params=params(),
        name="pack",
    )(
        vel, rate, weight, cell,
        volume_frac, volume_frac, velocity, volume_frac, volume_frac, velocity,
    )


def slot_table(block_sm, owner_sm, table, count, drops, members):
    def clear_count(i, _):
        count[i] = 0
        return 0

    def clear_table(i, _):
        table[i] = -1
        return 0

    lax.fori_loop(0, members, clear_count, 0)
    lax.fori_loop(0, members * CAP, clear_table, 0)

    def enter(j, _):
        owner = owner_sm[j]
        place = count[owner]
        count[owner] = place + 1
        table[owner * CAP + place] = block_sm[j]
        return 0

    lax.fori_loop(0, drops, enter, 0)


def rows_of_cell(cell):
    high = lax.shift_right_logical(cell, 4)
    rows = lax.broadcasted_iota(jnp.int32, (EDGE * EDGE, cell.shape[-1]), 0)
    return jnp.where(rows == high, 1.0, 0.0).astype(BF16)


def sample_body(
    blocks_y, blocks_z, block_sm, owner_sm, parcels_ref, frac_hbm, velocity_hbm, out_ref,
    speeds, fracs, table, count, sems,
):
    members = parcels_ref.shape[0]
    drops = block_sm.shape[0]
    slot_table(block_sm, owner_sm, table, count, drops, members)

    def copies(slot):
        block = jnp.maximum(table[slot], 0)
        bx = block // (blocks_y * blocks_z)
        by = block // blocks_z % blocks_y
        bz = block % blocks_z
        x = bx * EDGE
        y = pl.multiple_of(by * EDGE, EDGE)
        z = pl.multiple_of(bz * EDGE // LANES * LANES, LANES)
        return (
            pltpu.make_async_copy(
                velocity_hbm.at[:, pl.ds(x, EDGE), pl.ds(y, EDGE), pl.ds(z, LANES)],
                speeds.at[slot], sems.at[slot, 0],
            ),
            pltpu.make_async_copy(
                frac_hbm.at[pl.ds(x, EDGE), pl.ds(y, EDGE), pl.ds(z, LANES)],
                fracs.at[slot], sems.at[slot, 1],
            ),
        )

    def begin(slot, _):
        for copy in copies(slot):
            copy.start()
        return 0

    lax.fori_loop(0, members * CAP, begin, 0)

    parcels = parcels_ref.shape[-1]

    def sample(slot, member, place):
        for copy in copies(slot):
            copy.wait()
        block = table[slot]
        shift = block % blocks_z * EDGE % LANES
        cell = parcels_ref[member, 5, place:place + 1, :].astype(jnp.int32)
        third = jnp.bitwise_and(cell, EDGE - 1)
        tile = jnp.concatenate(
            [speeds[slot, k].reshape(EDGE * EDGE, LANES) for k in range(3)]
            + [fracs[slot].reshape(EDGE * EDGE, LANES).astype(BF16)],
            axis=1,
        )
        row = lax.broadcasted_iota(jnp.int32, (4 * EDGE, 4 * LANES), 0)
        column = lax.broadcasted_iota(jnp.int32, (4 * EDGE, 4 * LANES), 1)
        wanted = row // EDGE * LANES + row % EDGE + shift
        picker = jnp.where(column == wanted, 1.0, 0.0).astype(BF16)
        window = lax.dot_general(
            picker, tile, (((1,), (1,)), ((), ())), preferred_element_type=F32
        ).astype(BF16)
        spread = jnp.dot(window, rows_of_cell(cell), preferred_element_type=F32)
        lane = lax.broadcasted_iota(jnp.int32, (EDGE, parcels), 0)
        mask = lane == third
        picked = [
            jnp.sum(
                jnp.where(mask, spread[k * EDGE:(k + 1) * EDGE], 0.0), axis=0, keepdims=True
            )
            for k in range(4)
        ]
        filled = block >= 0
        return [jnp.where(filled, value, 0.0) for value in picked[:3]] + [
            jnp.where(filled, picked[3], 1.0)
        ]

    def one_member(member, _):
        first = sample(member * CAP, member, 0)
        second = sample(member * CAP + 1, member, 1)
        rows = [value for pair in zip(first, second) for value in pair]
        out_ref[member] = jnp.concatenate(rows, axis=0).astype(BF16)
        return 0

    lax.fori_loop(0, members, one_member, 0)


def sample_blocks(block_ids, owners, parcels, volume_frac, velocity):
    nx, ny, nz = volume_frac.shape
    members, _, _, count = parcels.shape
    slots = members * CAP
    return pl.pallas_call(
        functools.partial(sample_body, ny // EDGE, nz // EDGE),
        in_specs=[
            pl.BlockSpec(memory_space=pltpu.SMEM),
            pl.BlockSpec(memory_space=pltpu.SMEM),
            pl.BlockSpec(memory_space=pltpu.VMEM),
            pl.BlockSpec(memory_space=pl.ANY),
            pl.BlockSpec(memory_space=pl.ANY),
        ],
        out_specs=pl.BlockSpec(memory_space=pltpu.VMEM),
        out_shape=jax.ShapeDtypeStruct((members, 4 * CAP, count), BF16),
        scratch_shapes=[
            pltpu.VMEM((slots, 3, EDGE, EDGE, LANES), BF16),
            pltpu.VMEM((slots, EDGE, EDGE, LANES), F32),
            pltpu.SMEM((slots,), jnp.int32),
            pltpu.SMEM((members,), jnp.int32),
            pltpu.SemaphoreType.DMA((slots, 2)),
        ],
        compiler_params=params(),
        name="sample",
    )(block_ids, owners, parcels, volume_frac, velocity)


def advance_body(
    blocks_y, blocks_z,
    block_sm, owner_sm, parcels_ref, sampled_ref,
    frac_ref, frac_below, frac_above, speed_below, halo_below_x, halo_above_x,
    halo_below_y, halo_above_y, vel_ref,
    frac_out, vel_out,
    table, count, sides,
):
    step = pl.program_id(0)
    steps = pl.num_programs(0)
    members = parcels_ref.shape[0]
    drops = block_sm.shape[0]
    depth, ny, nz = frac_ref.shape

    @pl.when(step == 0)
    def _():
        slot_table(block_sm, owner_sm, table, count, drops, members)

    vel_out[...] = vel_ref[...]
    sides[0:2] = halo_below_y[...].astype(F32)
    sides[2:3] = halo_above_y[...].astype(F32)

    row8 = lax.broadcasted_iota(jnp.int32, (8, nz), 0)
    lane = lax.broadcasted_iota(jnp.int32, (ny, nz), 1)

    def flux(speed, lower, upper):
        return speed * jnp.where(speed > 0.0, lower, upper)

    first = step == 0
    last = step == steps - 1
    f_below = jnp.where(first, halo_below_x[0].astype(F32), frac_below[0])
    u_below = jnp.where(first, halo_below_x[1], speed_below[0, 0]).astype(F32)
    f_above = jnp.where(last, halo_above_x[0].astype(F32), frac_above[0])

    def layer(x, flux_low):
        f = frac_ref[x]
        u = vel_ref[0, x].astype(F32)
        v = vel_ref[1, x].astype(F32)
        w = vel_ref[2, x].astype(F32)
        f_up = jnp.where(x == depth - 1, f_above, frac_ref[jnp.minimum(x + 1, depth - 1)])
        flux_x = flux(u, f, f_up)
        up = pltpu.roll(f, ny - 1, 0)
        top = jnp.where(row8 == 7, sides[2, pl.ds(x, 1), :], up[ny - 8:])
        up = jnp.concatenate([up[:ny - 8], top], axis=0)
        flux_y = flux(v, f, up)
        edge = flux(sides[1, pl.ds(x, 1), :], sides[0, pl.ds(x, 1), :], f[0:1])
        down = pltpu.roll(flux_y, 1, 0)
        low = jnp.where(row8 == 0, edge, down[:8])
        down = jnp.concatenate([low, down[8:]], axis=0)
        right = jnp.where(lane == nz - 1, 0.0, pltpu.roll(f, nz - 1, 1))
        flux_z = flux(w, f, right)
        left = jnp.where(lane == 0, 0.0, pltpu.roll(flux_z, 1, 1))
        change = (flux_x - flux_low) + (flux_y - down) + (flux_z - left)
        frac_out[x] = jnp.minimum(f - courant * change, 1.0)
        return flux_x

    lax.fori_loop(0, depth, layer, flux(u_below, f_below, frac_ref[0]))

    parcels = parcels_ref.shape[-1]

    def place(slot, _):
        block = table[slot]

        @pl.when((block >= 0) & (block // (blocks_y * blocks_z) == step))
        def _():
            member = slot // CAP
            odd = slot % CAP == 1
            by = block // blocks_z % blocks_y
            bz = block % blocks_z
            y = pl.multiple_of(by * EDGE, EDGE)
            z = pl.multiple_of(bz * EDGE // LANES * LANES, LANES)
            shift = bz * EDGE % LANES

            def field(k):
                both = parcels_ref[member, k]
                return jnp.where(odd, both[1:2], both[0:1])

            got = sampled_ref[member].astype(F32)

            def value(k):
                return jnp.where(odd, got[2 * k + 1:2 * k + 2], got[2 * k:2 * k + 1])

            cell = field(5).astype(jnp.int32)
            factor = field(3) * (1.0 - value(3))
            weight = field(4)
            hits = lax.broadcasted_iota(jnp.int32, (LANES, parcels), 0) == (
                jnp.bitwise_and(cell, EDGE - 1) + shift
            )
            deposits = jnp.concatenate(
                [
                    jnp.where(hits, weight * (factor * (value(k) - field(k))), 0.0).astype(BF16)
                    for k in range(3)
                ],
                axis=0,
            )
            source = lax.dot_general(
                rows_of_cell(cell), deposits, (((1,), (1,)), ((), ())),
                preferred_element_type=F32,
            )
            for k in range(3):
                spot = (k, slice(None), pl.ds(y, EDGE), pl.ds(z, LANES))
                added = source[:, k * LANES:(k + 1) * LANES].astype(BF16).astype(F32)
                old = vel_out[spot].astype(F32).reshape(EDGE * EDGE, LANES)
                vel_out[spot] = (old + added).astype(BF16).reshape(EDGE, EDGE, LANES)

        return 0

    lax.fori_loop(0, members * CAP, place, 0)


def advance(block_ids, owners, parcels, sampled, volume_frac, velocity, below_x, above_x, below_y, above_y):
    nx, ny, nz = volume_frac.shape
    members = parcels.shape[0]
    depth = EDGE
    steps = nx // depth
    return pl.pallas_call(
        functools.partial(advance_body, ny // EDGE, nz // EDGE),
        grid=(steps,),
        in_specs=[
            pl.BlockSpec(memory_space=pltpu.SMEM),
            pl.BlockSpec(memory_space=pltpu.SMEM),
            whole(parcels.shape),
            whole(sampled.shape),
            pl.BlockSpec((depth, ny, nz), lambda i: (i, 0, 0)),
            pl.BlockSpec((1, ny, nz), lambda i: (jnp.maximum(i * depth - 1, 0), 0, 0)),
            pl.BlockSpec((1, ny, nz), lambda i: (jnp.minimum((i + 1) * depth, nx - 1), 0, 0)),
            pl.BlockSpec((1, 1, ny, nz), lambda i: (0, jnp.maximum(i * depth - 1, 0), 0, 0)),
            whole(below_x.shape),
            whole(above_x.shape),
            pl.BlockSpec((2, depth, nz), lambda i: (0, i, 0)),
            pl.BlockSpec((1, depth, nz), lambda i: (0, i, 0)),
            pl.BlockSpec((3, depth, ny, nz), lambda i: (0, i, 0, 0)),
        ],
        out_specs=[
            pl.BlockSpec((depth, ny, nz), lambda i: (i, 0, 0)),
            pl.BlockSpec((3, depth, ny, nz), lambda i: (0, i, 0, 0)),
        ],
        out_shape=[
            jax.ShapeDtypeStruct(volume_frac.shape, F32),
            jax.ShapeDtypeStruct(velocity.shape, BF16),
        ],
        scratch_shapes=[
            pltpu.SMEM((members * CAP,), jnp.int32),
            pltpu.SMEM((members,), jnp.int32),
            pltpu.VMEM((3, depth, nz), F32),
        ],
        compiler_params=params(),
        name="advance",
    )(
        block_ids, owners, parcels, sampled,
        volume_frac, volume_frac, volume_frac, velocity, below_x, above_x, below_y, above_y,
        velocity,
    )


def drag_body(vel_ref, rate_ref, sampled_ref, out_ref):
    members = vel_ref.shape[0]
    for member in range(members):
        got = sampled_ref[member].astype(F32)
        factor = rate_ref[member] * (1.0 - got[3 * CAP:4 * CAP])
        for k in range(3):
            old = vel_ref[member, k]
            out_ref[member, k] = old + factor * (got[k * CAP:(k + 1) * CAP] - old)


def drag(vel, rate, sampled):
    return pl.pallas_call(
        drag_body,
        out_shape=jax.ShapeDtypeStruct(vel.shape, F32),
        compiler_params=params(),
        name="drag",
    )(vel, rate, sampled)


def per_device(
    volume_frac,
    velocity,
    drop_block,
    drop_owner,
    parcel_vel,
    parcel_rate,
    parcel_weight,
    parcel_cell,
):
    block_ids = drop_block.reshape(-1)
    owners = drop_owner.reshape(-1)
    vel = jnp.swapaxes(parcel_vel[0, 0], 1, 2)
    rate = parcel_rate[0, 0]
    parcels, up_x, down_x, up_y, down_y = pack(
        volume_frac, velocity, vel, rate, parcel_weight[0, 0], parcel_cell[0, 0]
    )
    parcels_in = lax.all_to_all(parcels, "member", split_axis=0, concat_axis=0, tiled=True)
    below_x = passed_along(up_x, "group", 1)
    above_x = passed_along(down_x, "group", -1)
    below_y = passed_along(up_y, "member", 1)
    above_y = passed_along(down_y, "member", -1)
    sampled = sample_blocks(block_ids, owners, parcels_in, volume_frac, velocity)
    returned = lax.all_to_all(sampled, "member", split_axis=0, concat_axis=0, tiled=True)
    frac_next, velocity_next = advance(
        block_ids, owners, parcels_in, sampled, volume_frac, velocity,
        below_x, above_x, below_y, above_y,
    )
    vel_next = drag(vel, rate, returned)
    parcel_next = jnp.swapaxes(vel_next, 1, 2)[None, None]
    return (frac_next, velocity_next, parcel_next)


def solution(mesh):
    in_specs = (
        P("group", "member", None),
        P(None, "group", "member", None),
        P("group", "member", None),
        P("group", "member", None, None),
        P("group", "member", None, None, None, None),
        P("group", "member", None, None, None),
        P("group", "member", None, None, None),
        P("group", "member", None, None, None),
    )
    out_specs = (
        P("group", "member", None),
        P(None, "group", "member", None),
        P("group", "member", None, None, None, None),
    )
    return jax.shard_map(
        per_device, mesh=mesh, in_specs=in_specs, out_specs=out_specs, check_vma=False
    )
```

```python
import functools

import jax
import jax.numpy as jnp
from jax import lax
from jax.experimental import pallas as pl
from jax.experimental.pallas import tpu as pltpu
from jax.sharding import PartitionSpec as P

CAP = 2
EDGE = 16
LANES = 128
FIELDS = 6
GROUP = 2

courant = 0.025

F32 = jnp.float32
BF16 = jnp.bfloat16


def passed_around(block, axis, distance):
    size = lax.axis_size(axis)
    return lax.ppermute(block, axis, [(i, (i + distance) % size) for i in range(size)])


def whole(shape):
    return pl.BlockSpec(shape, lambda *_: (0,) * len(shape))


def params(**more):
    return pltpu.CompilerParams(vmem_limit_bytes=24 * 1024 * 1024, **more)


def pack_body(
    vel_ref, rate_ref, weight_ref, cell_ref,
    f_first_x, f_last_x, u_last_x, f_first_y, f_last_y, u_last_y,
    parcels_ref, up_x, down_x, up_y, down_y,
):
    parcels_ref[:, 0:3] = vel_ref[...]
    parcels_ref[:, 3] = rate_ref[...]
    parcels_ref[:, 4] = weight_ref[...]
    parcels_ref[:, 5] = cell_ref[...].astype(F32)
    up_x[0] = f_last_x[0].astype(BF16)
    up_x[1] = u_last_x[0, 0]
    down_x[0] = f_first_x[0].astype(BF16)
    up_y[0] = f_last_y[:, 7, :].astype(BF16)
    up_y[1] = u_last_y[0].astype(F32)[:, 15, :].astype(BF16)
    down_y[0] = f_first_y[:, 0, :].astype(BF16)


def pack(volume_frac, velocity, vel, rate, weight, cell):
    nx, ny, nz = volume_frac.shape
    members, _, parcels = rate.shape
    return pl.pallas_call(
        pack_body,
        grid=(1,),
        in_specs=[
            whole(vel.shape),
            whole(rate.shape),
            whole(weight.shape),
            whole(cell.shape),
            pl.BlockSpec((1, ny, nz), lambda i: (0, 0, 0)),
            pl.BlockSpec((1, ny, nz), lambda i: (nx - 1, 0, 0)),
            pl.BlockSpec((1, 1, ny, nz), lambda i: (0, nx - 1, 0, 0)),
            pl.BlockSpec((nx, 8, nz), lambda i: (0, 0, 0)),
            pl.BlockSpec((nx, 8, nz), lambda i: (0, ny // 8 - 1, 0)),
            pl.BlockSpec((1, nx, 16, nz), lambda i: (1, 0, ny // 16 - 1, 0)),
        ],
        out_specs=[
            whole((members, FIELDS, CAP, parcels)),
            whole((2, ny, nz)),
            whole((1, ny, nz)),
            whole((2, nx, nz)),
            whole((1, nx, nz)),
        ],
        out_shape=[
            jax.ShapeDtypeStruct((members, FIELDS, CAP, parcels), F32),
            jax.ShapeDtypeStruct((2, ny, nz), BF16),
            jax.ShapeDtypeStruct((1, ny, nz), BF16),
            jax.ShapeDtypeStruct((2, nx, nz), BF16),
            jax.ShapeDtypeStruct((1, nx, nz), BF16),
        ],
        compiler_params=params(),
        name="pack",
    )(
        *in_hbm(vel, rate, weight, cell),
        *in_hbm(volume_frac, volume_frac, velocity, volume_frac, volume_frac, velocity),
    )


def slot_table(block_sm, owner_sm, table, count, drops, members):
    def clear_count(i, _):
        count[i] = 0
        return 0

    def clear_table(i, _):
        table[i] = -1
        return 0

    lax.fori_loop(0, members, clear_count, 0)
    lax.fori_loop(0, members * CAP, clear_table, 0)

    def enter(j, _):
        owner = owner_sm[j]
        place = count[owner]
        count[owner] = place + 1
        table[owner * CAP + place] = block_sm[j]
        return 0

    lax.fori_loop(0, drops, enter, 0)


def corner(block, blocks_y, blocks_z):
    x = block // (blocks_y * blocks_z) * EDGE
    y = pl.multiple_of(block // blocks_z % blocks_y * EDGE, EDGE)
    z = block % blocks_z * EDGE
    return x, y, pl.multiple_of(z // LANES * LANES, LANES), z % LANES


def rows_of_cell(cell):
    high = lax.shift_right_logical(cell, 4)
    rows = lax.broadcasted_iota(jnp.int32, (EDGE * EDGE, cell.shape[-1]), 0)
    return jnp.where(rows == high, 1.0, 0.0).astype(BF16)


def window_of(shift, velocity_ref, frac_ref, spot):
    tile = jnp.concatenate(
        [velocity_ref[(k,) + spot].reshape(EDGE * EDGE, LANES) for k in range(3)]
        + [frac_ref[spot].reshape(EDGE * EDGE, LANES).astype(BF16)],
        axis=1,
    )
    row = lax.broadcasted_iota(jnp.int32, (4 * EDGE, 4 * LANES), 0)
    column = lax.broadcasted_iota(jnp.int32, (4 * EDGE, 4 * LANES), 1)
    wanted = row // EDGE * LANES + row % EDGE + shift
    picker = jnp.where(column == wanted, 1.0, 0.0).astype(BF16)
    return lax.dot_general(
        picker, tile, (((1,), (1,)), ((), ())), preferred_element_type=F32
    ).astype(BF16)


def advect_body(
    blocks_y, blocks_z,
    block_sm, owner_sm, edge_sm,
    halo_below_x, halo_above_x, halo_below_y, halo_above_y, frac_hbm, vel_hbm,
    frac_next, windows_ref,
    table, count, frac_ref, vel_ref, frac_out, sides, flux_low,
    right_even, right_odd, third_even, third_odd, rest_even, rest_odd, sems,
):
    members = count.shape[0]
    drops = block_sm.shape[0]
    nx, ny, nz = frac_out.shape
    steps = sems.shape[1]
    depth = nx // steps
    chunk = right_even.shape[0]

    def part(step):
        return pl.ds(step * depth, depth)

    def frac_in(step):
        return pltpu.make_async_copy(
            frac_hbm.at[part(step)], frac_ref.at[part(step)], sems.at[0, step]
        )

    def vel_in(step):
        return pltpu.make_async_copy(
            vel_hbm.at[:, part(step)], vel_ref.at[:, part(step)], sems.at[1, step]
        )

    def frac_copy(step):
        return pltpu.make_async_copy(
            frac_out.at[part(step)], frac_next.at[part(step)], sems.at[2, step]
        )

    frac_in(0).start()
    for step in range(steps):
        vel_in(step).start()
        if step + 1 < steps:
            frac_in(step + 1).start()

    slot_table(block_sm, owner_sm, table, count, drops, members)

    inner = [edge_sm[i].astype(F32) for i in range(4)]
    frac_ref[nx] = halo_above_x[0].astype(F32) * inner[1]
    sides[0:2] = halo_below_y[...].astype(F32) * inner[2]
    sides[2:3] = halo_above_y[...].astype(F32) * inner[3]
    row = lax.broadcasted_iota(jnp.int32, (8, LANES), 0)
    row_last, row_first = row == 7, row == 0
    along = lax.broadcasted_iota(jnp.int32, (nz, nz), 0)
    across = lax.broadcasted_iota(jnp.int32, (nz, nz), 1)
    shift_left = jnp.where(along == across + 1, 1.0, 0.0).astype(BF16)
    difference = jnp.where(
        along == across, 1.0, jnp.where(along + 1 == across, -1.0, 0.0)
    ).astype(BF16)

    def flux(speed, lower, upper):
        return speed * jnp.where(speed > 0, lower, upper)

    frac_in(0).wait()
    flux_low[...] = flux(
        halo_below_x[1].astype(F32) * inner[0], halo_below_x[0].astype(F32), frac_ref[0]
    )

    def look_right(piece, right):
        cells = frac_ref[pl.ds(piece * chunk, chunk)].reshape(chunk * ny, nz).astype(BF16)
        right[...] = jnp.dot(cells, shift_left, preferred_element_type=F32).reshape(
            chunk, ny, nz
        )

    def finish(piece, third, rest):
        change = jnp.dot(
            third[...].reshape(chunk * ny, nz), difference, preferred_element_type=F32
        ).reshape(chunk, ny, nz)
        frac_out[pl.ds(piece * chunk, chunk)] = jnp.minimum(rest[...] - courant * change, 1.0)

    def layer(x, level, right, third, rest):
        side = sides[:, pl.ds(x, 1), :]
        for h in range(nz // LANES):
            lanes = slice(LANES * h, LANES * h + LANES)
            here = frac_ref[x, 0:8, lanes]
            edge = flux(side[1, :, lanes], side[0, :, lanes], here[0:1])
            carried = jnp.broadcast_to(edge, (8, LANES))
            turned_f = pltpu.roll(here, 7, 0)
            for p in range(ny // 16):
                pair = slice(16 * p, 16 * p + 16)
                u = vel_ref[0, x, pair, lanes].astype(F32)
                v = vel_ref[1, x, pair, lanes].astype(F32)
                w = vel_ref[2, x, pair, lanes]
                both = frac_ref[x, pair, lanes]
                third[level, pair, lanes] = flux(
                    w, both.astype(BF16), right[level, pair, lanes].astype(BF16)
                )
                for t in (2 * p, 2 * p + 1):
                    rows = slice(8 * t, 8 * t + 8)
                    half = slice(8 * (t % 2), 8 * (t % 2) + 8)
                    here = both[half]
                    out_x = flux(u[half], here, frac_ref[x + 1, rows, lanes])
                    change = out_x - flux_low[rows, lanes]
                    flux_low[rows, lanes] = out_x
                    if t + 1 < ny // 8:
                        following = frac_ref[x, 8 * t + 8:8 * t + 16, lanes]
                        turned_next = pltpu.roll(following, 7, 0)
                    else:
                        turned_next = jnp.broadcast_to(side[2, :, lanes], (8, LANES))
                    up = jnp.where(row_last, turned_next, turned_f)
                    turned_f = turned_next
                    out_y = flux(v[half], here, up)
                    rolled = pltpu.roll(out_y, 1, 0)
                    change = change + (out_y - jnp.where(row_first, carried, rolled))
                    carried = rolled
                    rest[level, rows, lanes] = here - courant * change

    pieces = depth // chunk
    total = nx // chunk
    look_right(0, right_even)

    def one_step(step, _):
        vel_in(step).wait()

        @pl.when(step + 1 < steps)
        def _():
            frac_in(step + 1).wait()

        first = step * pieces
        even = (right_even, third_even, rest_even)
        odd = (right_odd, third_odd, rest_odd)
        for k in range(pieces):
            now, other = (even, odd) if k % 2 == 0 else (odd, even)
            look_right(jnp.minimum(first + k + 1, total - 1), other[0])
            finish(jnp.maximum(first + k - 1, 0), other[1], other[2])
            for level in range(chunk):
                layer((first + k) * chunk + level, level, *now)

        @pl.when(step > 0)
        def _():
            frac_copy(step - 1).start()

        return 0

    lax.fori_loop(0, steps, one_step, 0)
    finish(total - 1, third_odd, rest_odd)
    frac_copy(steps - 1).start()

    def some_windows(first, _):
        for more in range(GROUP * CAP):
            slot = first * GROUP * CAP + more
            x, y, z, shift = corner(jnp.maximum(table[slot], 0), blocks_y, blocks_z)
            spot = (pl.ds(x, EDGE), pl.ds(y, EDGE), pl.ds(z, LANES))
            windows_ref[slot] = window_of(shift, vel_ref, frac_ref, spot)
        return 0

    lax.fori_loop(0, members // GROUP, some_windows, 0)

    for step in range(steps):
        frac_copy(step).wait()


def in_hbm(*arrays):
    return [pltpu.with_memory_space_constraint(array, pltpu.HBM) for array in arrays]


def advect(block_ids, owners, edges, volume_frac, velocity, below_x, above_x, below_y, above_y, members):
    nx, ny, nz = volume_frac.shape
    slots = members * CAP
    steps = nx // 8
    chunk = 4
    return pl.pallas_call(
        functools.partial(advect_body, ny // EDGE, nz // EDGE),
        in_specs=[pl.BlockSpec(memory_space=pltpu.SMEM)] * 3
        + [pl.BlockSpec(memory_space=pltpu.VMEM)] * 4
        + [pl.BlockSpec(memory_space=pltpu.HBM)] * 2,
        out_specs=[
            pl.BlockSpec(memory_space=pltpu.HBM),
            pl.BlockSpec(memory_space=pltpu.VMEM),
        ],
        out_shape=[
            jax.ShapeDtypeStruct(volume_frac.shape, F32),
            jax.ShapeDtypeStruct((slots, 4 * EDGE, EDGE * EDGE), BF16),
        ],
        scratch_shapes=[
            pltpu.SMEM((slots,), jnp.int32),
            pltpu.SMEM((members,), jnp.int32),
            pltpu.VMEM((nx + 1, ny, nz), F32),
            pltpu.VMEM(velocity.shape, BF16),
            pltpu.VMEM(volume_frac.shape, F32),
            pltpu.VMEM((3, nx, nz), F32),
            pltpu.VMEM((ny, nz), F32),
            pltpu.VMEM((chunk, ny, nz), F32),
            pltpu.VMEM((chunk, ny, nz), F32),
            pltpu.VMEM((chunk, ny, nz), BF16),
            pltpu.VMEM((chunk, ny, nz), BF16),
            pltpu.VMEM((chunk, ny, nz), F32),
            pltpu.VMEM((chunk, ny, nz), F32),
            pltpu.SemaphoreType.DMA((3, steps)),
        ],
        compiler_params=params(),
        name="advect",
    )(
        block_ids, owners, edges, below_x, above_x, below_y, above_y,
        *in_hbm(volume_frac, velocity),
    )


def sample_body(block_sm, owner_sm, parcels_ref, windows_ref, out_ref, table, count):
    members = parcels_ref.shape[0]
    parcels = parcels_ref.shape[-1]
    slot_table(block_sm, owner_sm, table, count, block_sm.shape[0], members)

    def sample(slot, member, place):
        cell = parcels_ref[member, 5, place:place + 1, :].astype(jnp.int32)
        spread = jnp.dot(windows_ref[slot], rows_of_cell(cell), preferred_element_type=F32)
        mask = lax.broadcasted_iota(jnp.int32, (EDGE, parcels), 0) == jnp.bitwise_and(
            cell, EDGE - 1
        )
        picked = [
            jnp.sum(
                jnp.where(mask, spread[k * EDGE:(k + 1) * EDGE], 0.0), axis=0, keepdims=True
            )
            for k in range(4)
        ]
        filled = table[slot] >= 0
        return [jnp.where(filled, value, 0.0) for value in picked[:3]] + [
            jnp.where(filled, picked[3], 1.0)
        ]

    def some_members(first_member, _):
        for more in range(GROUP):
            member = first_member * GROUP + more
            first = sample(member * CAP, member, 0)
            second = sample(member * CAP + 1, member, 1)
            rows = [value for pair in zip(first, second) for value in pair]
            out_ref[member] = jnp.concatenate(rows, axis=0).astype(BF16)
        return 0

    lax.fori_loop(0, members // GROUP, some_members, 0)


def sample_parcels(block_ids, owners, parcels, windows):
    members, _, _, count = parcels.shape
    return pl.pallas_call(
        sample_body,
        in_specs=[pl.BlockSpec(memory_space=pltpu.SMEM)] * 2
        + [pl.BlockSpec(memory_space=pltpu.VMEM)] * 2,
        out_specs=pl.BlockSpec(memory_space=pltpu.VMEM),
        out_shape=jax.ShapeDtypeStruct((members, 4 * CAP, count), BF16),
        scratch_shapes=[
            pltpu.SMEM((members * CAP,), jnp.int32),
            pltpu.SMEM((members,), jnp.int32),
        ],
        compiler_params=params(),
        name="sample",
    )(block_ids, owners, parcels, windows)


def source_body(
    blocks_y, blocks_z, block_sm, owner_sm, parcels_ref, sampled_ref, vel_hbm,
    vel_next,
    table, count, vel_out, sources, sems,
):
    members = parcels_ref.shape[0]
    parcels = parcels_ref.shape[-1]
    drops = block_sm.shape[0]
    steps = sems.shape[1]
    depth = EDGE

    def vel_in(step):
        part = pl.ds(step * depth, depth)
        return pltpu.make_async_copy(
            vel_hbm.at[:, part], vel_out.at[:, part], sems.at[0, step]
        )

    def vel_copy(step):
        part = pl.ds(step * depth, depth)
        return pltpu.make_async_copy(
            vel_out.at[:, part], vel_next.at[:, part], sems.at[1, step]
        )

    for step in range(steps):
        vel_in(step).start()
    slot_table(block_sm, owner_sm, table, count, drops, members)

    def source_of(slot, member, place):
        block = table[slot]
        shift = corner(jnp.maximum(block, 0), blocks_y, blocks_z)[3]

        def field(k):
            return parcels_ref[member, k, place:place + 1, :]

        got = sampled_ref[member].astype(F32)

        def value(k):
            return got[2 * k + place:2 * k + place + 1]

        cell = field(5).astype(jnp.int32)
        factor = field(3) * (1.0 - value(3))
        weight = field(4)
        wanted = jnp.where(block >= 0, jnp.bitwise_and(cell, EDGE - 1) + shift, -1)
        hits = lax.broadcasted_iota(jnp.int32, (LANES, parcels), 0) == wanted
        deposits = jnp.concatenate(
            [
                jnp.where(hits, weight * (factor * (value(k) - field(k))), 0.0).astype(BF16)
                for k in range(3)
            ],
            axis=0,
        )
        source = lax.dot_general(
            rows_of_cell(cell), deposits, (((1,), (1,)), ((), ())), preferred_element_type=F32
        )
        sources[slot] = source.astype(BF16)

    def some_members(first_member, _):
        for more in range(GROUP):
            member = first_member * GROUP + more
            for place in range(CAP):
                source_of(member * CAP + place, member, place)
        return 0

    lax.fori_loop(0, members // GROUP, some_members, 0)
    for step in range(steps):
        vel_in(step).wait()

    def add_source(slot, _):
        x, y, z, _ = corner(jnp.maximum(table[slot], 0), blocks_y, blocks_z)
        for k in range(3):
            here = (k, pl.ds(x, EDGE), pl.ds(y, EDGE), pl.ds(z, LANES))
            added = sources[slot, :, k * LANES:(k + 1) * LANES].astype(F32)
            old = vel_out[here].astype(F32).reshape(EDGE * EDGE, LANES)
            vel_out[here] = (old + added).astype(BF16).reshape(EDGE, EDGE, LANES)
        return 0

    lax.fori_loop(0, members * CAP, add_source, 0)
    for step in range(steps):
        vel_copy(step).start()
    for step in range(steps):
        vel_copy(step).wait()


def add_drag(block_ids, owners, parcels, sampled, velocity):
    _, nx, ny, nz = velocity.shape
    members = parcels.shape[0]
    slots = members * CAP
    return pl.pallas_call(
        functools.partial(source_body, ny // EDGE, nz // EDGE),
        in_specs=[pl.BlockSpec(memory_space=pltpu.SMEM)] * 2
        + [pl.BlockSpec(memory_space=pltpu.VMEM)] * 2
        + [pl.BlockSpec(memory_space=pltpu.HBM)],
        out_specs=pl.BlockSpec(memory_space=pltpu.HBM),
        out_shape=jax.ShapeDtypeStruct(velocity.shape, BF16),
        scratch_shapes=[
            pltpu.SMEM((slots,), jnp.int32),
            pltpu.SMEM((members,), jnp.int32),
            pltpu.VMEM(velocity.shape, BF16),
            pltpu.VMEM((slots, EDGE * EDGE, 3 * LANES), BF16),
            pltpu.SemaphoreType.DMA((2, nx // EDGE)),
        ],
        compiler_params=params(),
        name="add_drag",
    )(block_ids, owners, parcels, sampled, *in_hbm(velocity))


def drag_body(vel_ref, rate_ref, sampled_ref, out_ref):
    members = vel_ref.shape[0]
    for member in range(members):
        got = sampled_ref[member].astype(F32)
        factor = rate_ref[member] * (1.0 - got[3 * CAP:4 * CAP])
        for k in range(3):
            old = vel_ref[member, k]
            out_ref[member, k] = old + factor * (got[k * CAP:(k + 1) * CAP] - old)


def drag(vel, rate, sampled):
    return pl.pallas_call(
        drag_body,
        out_shape=jax.ShapeDtypeStruct(vel.shape, F32),
        compiler_params=params(),
        name="drag",
    )(vel, rate, sampled)


def per_device(
    volume_frac,
    velocity,
    drop_block,
    drop_owner,
    parcel_vel,
    parcel_rate,
    parcel_weight,
    parcel_cell,
):
    block_ids = drop_block.reshape(-1)
    owners = drop_owner.reshape(-1)
    vel = jnp.swapaxes(parcel_vel[0, 0], 1, 2)
    rate = parcel_rate[0, 0]
    parcels, up_x, down_x, up_y, down_y = pack(
        volume_frac, velocity, vel, rate, parcel_weight[0, 0], parcel_cell[0, 0]
    )
    below_x = passed_around(up_x, "group", 1)
    above_x = passed_around(down_x, "group", -1)
    below_y = passed_around(up_y, "member", 1)
    above_y = passed_around(down_y, "member", -1)
    parcels_in = lax.all_to_all(parcels, "member", split_axis=0, concat_axis=0, tiled=True)
    edges = jnp.stack(
        [
            lax.axis_index("group") > 0,
            lax.axis_index("group") < lax.axis_size("group") - 1,
            lax.axis_index("member") > 0,
            lax.axis_index("member") < lax.axis_size("member") - 1,
        ]
    ).astype(jnp.int32)
    frac_next, windows = advect(
        block_ids, owners, edges, volume_frac, velocity,
        below_x, above_x, below_y, above_y, rate.shape[0],
    )
    parcels_in, windows = lax.optimization_barrier((parcels_in, windows))
    sampled = sample_parcels(block_ids, owners, parcels_in, windows)
    returned = lax.all_to_all(sampled, "member", split_axis=0, concat_axis=0, tiled=True)
    velocity_next = add_drag(block_ids, owners, parcels_in, sampled, velocity)
    vel_next = drag(vel, rate, returned)
    parcel_next = jnp.swapaxes(vel_next, 1, 2)[None, None]
    return (frac_next, velocity_next, parcel_next)


def solution(mesh):
    in_specs = (
        P("group", "member", None),
        P(None, "group", "member", None),
        P("group", "member", None),
        P("group", "member", None, None),
        P("group", "member", None, None, None, None),
        P("group", "member", None, None, None),
        P("group", "member", None, None, None),
        P("group", "member", None, None, None),
    )
    out_specs = (
        P("group", "member", None),
        P(None, "group", "member", None),
        P("group", "member", None, None, None, None),
    )
    return jax.shard_map(
        per_device, mesh=mesh, in_specs=in_specs, out_specs=out_specs, check_vma=False
    )
```

```python
import functools

import jax
import jax.numpy as jnp
from jax import lax
from jax.experimental import pallas as pl
from jax.experimental.pallas import tpu as pltpu
from jax.sharding import PartitionSpec as P

CAP = 2
EDGE = 16
LANES = 128
FIELDS = 6
GROUP = 2

courant = 0.025

F32 = jnp.float32
BF16 = jnp.bfloat16


def passed_around(block, axis, distance):
    size = lax.axis_size(axis)
    return lax.ppermute(block, axis, [(i, (i + distance) % size) for i in range(size)])


def whole(shape):
    return pl.BlockSpec(shape, lambda *_: (0,) * len(shape))


def params(**more):
    return pltpu.CompilerParams(vmem_limit_bytes=24 * 1024 * 1024, **more)


def pack_body(
    vel_ref, rate_ref, weight_ref, cell_ref,
    f_first_x, f_last_x, u_last_x, f_first_y, f_last_y, u_last_y,
    parcels_ref, up_x, down_x, up_y, down_y,
):
    parcels_ref[:, 0:3] = vel_ref[...]
    parcels_ref[:, 3] = rate_ref[...]
    parcels_ref[:, 4] = weight_ref[...]
    parcels_ref[:, 5] = cell_ref[...].astype(F32)
    up_x[0] = f_last_x[0].astype(BF16)
    up_x[1] = u_last_x[0, 0]
    down_x[0] = f_first_x[0].astype(BF16)
    up_y[0] = f_last_y[:, 7, :].astype(BF16)
    up_y[1] = u_last_y[0].astype(F32)[:, 15, :].astype(BF16)
    down_y[0] = f_first_y[:, 0, :].astype(BF16)


def pack(volume_frac, velocity, vel, rate, weight, cell):
    nx, ny, nz = volume_frac.shape
    members, _, parcels = rate.shape
    return pl.pallas_call(
        pack_body,
        grid=(1,),
        in_specs=[
            whole(vel.shape),
            whole(rate.shape),
            whole(weight.shape),
            whole(cell.shape),
            pl.BlockSpec((1, ny, nz), lambda i: (0, 0, 0)),
            pl.BlockSpec((1, ny, nz), lambda i: (nx - 1, 0, 0)),
            pl.BlockSpec((1, 1, ny, nz), lambda i: (0, nx - 1, 0, 0)),
            pl.BlockSpec((nx, 8, nz), lambda i: (0, 0, 0)),
            pl.BlockSpec((nx, 8, nz), lambda i: (0, ny // 8 - 1, 0)),
            pl.BlockSpec((1, nx, 16, nz), lambda i: (1, 0, ny // 16 - 1, 0)),
        ],
        out_specs=[
            whole((members, FIELDS, CAP, parcels)),
            whole((2, ny, nz)),
            whole((1, ny, nz)),
            whole((2, nx, nz)),
            whole((1, nx, nz)),
        ],
        out_shape=[
            jax.ShapeDtypeStruct((members, FIELDS, CAP, parcels), F32),
            jax.ShapeDtypeStruct((2, ny, nz), BF16),
            jax.ShapeDtypeStruct((1, ny, nz), BF16),
            jax.ShapeDtypeStruct((2, nx, nz), BF16),
            jax.ShapeDtypeStruct((1, nx, nz), BF16),
        ],
        compiler_params=params(),
        name="pack",
    )(
        *in_hbm(vel, rate, weight, cell),
        *in_hbm(volume_frac, volume_frac, velocity, volume_frac, volume_frac, velocity),
    )


def slot_table(block_sm, owner_sm, table, count, drops, members):
    def clear_count(i, _):
        count[i] = 0
        return 0

    def clear_table(i, _):
        table[i] = -1
        return 0

    lax.fori_loop(0, members, clear_count, 0)
    lax.fori_loop(0, members * CAP, clear_table, 0)

    def enter(j, _):
        owner = owner_sm[j]
        place = count[owner]
        count[owner] = place + 1
        table[owner * CAP + place] = block_sm[j]
        return 0

    lax.fori_loop(0, drops, enter, 0)


def corner(block, blocks_y, blocks_z):
    x = block // (blocks_y * blocks_z) * EDGE
    y = pl.multiple_of(block // blocks_z % blocks_y * EDGE, EDGE)
    z = block % blocks_z * EDGE
    return x, y, pl.multiple_of(z // LANES * LANES, LANES), z % LANES


def rows_of_cell(cell):
    high = lax.shift_right_logical(cell, 4).astype(F32).astype(BF16)
    rows = lax.broadcasted_iota(jnp.int32, (EDGE * EDGE, cell.shape[-1]), 0)
    hits = rows.astype(F32).astype(BF16) == high
    return jnp.where(hits, jnp.ones_like(high), jnp.zeros_like(high))


def window_of(shift, velocity_ref, frac_ref, spot):
    tile = jnp.concatenate(
        [velocity_ref[(k,) + spot].reshape(EDGE * EDGE, LANES) for k in range(3)]
        + [frac_ref[spot].reshape(EDGE * EDGE, LANES).astype(BF16)],
        axis=1,
    )
    row = lax.broadcasted_iota(jnp.int32, (4 * EDGE, 4 * LANES), 0)
    column = lax.broadcasted_iota(jnp.int32, (4 * EDGE, 4 * LANES), 1)
    wanted = row // EDGE * LANES + row % EDGE + shift
    picker = jnp.where(column == wanted, 1.0, 0.0).astype(BF16)
    return lax.dot_general(
        picker, tile, (((1,), (1,)), ((), ())), preferred_element_type=F32
    ).astype(BF16)


def advect_body(
    blocks_y, blocks_z,
    block_hbm, owner_hbm, edge_sm,
    halo_below_x, halo_above_x, halo_below_y, halo_above_y, frac_hbm, vel_hbm,
    frac_next, windows_ref,
    block_sm, owner_sm, table, count, frac_ref, vel_ref, frac_out, sides, flux_low,
    right_even, right_odd, third_even, third_odd, rest_even, rest_odd, sems, scalar_sems,
):
    members = count.shape[0]
    drops = block_sm.shape[0]
    nx, ny, nz = frac_out.shape
    steps = sems.shape[1]
    depth = nx // steps
    chunk = right_even.shape[0]

    def part(step):
        return pl.ds(step * depth, depth)

    def frac_in(step):
        return pltpu.make_async_copy(
            frac_hbm.at[part(step)], frac_ref.at[part(step)], sems.at[0, step]
        )

    def vel_in(step):
        return [
            pltpu.make_async_copy(
                vel_hbm.at[k, part(step)], vel_ref.at[k, part(step)], sems.at[2 + k, step]
            )
            for k in range(3)
        ]

    def frac_copy(step):
        return pltpu.make_async_copy(
            frac_out.at[part(step)], frac_next.at[part(step)], sems.at[1, step]
        )

    frac_in(0).start()
    for step in range(steps):
        for copy in vel_in(step):
            copy.start()
        if step + 1 < steps:
            frac_in(step + 1).start()

    scalars = [
        pltpu.make_async_copy(block_hbm, block_sm, scalar_sems.at[0]),
        pltpu.make_async_copy(owner_hbm, owner_sm, scalar_sems.at[1]),
    ]
    for copy in scalars:
        copy.start()
    for copy in scalars:
        copy.wait()
    slot_table(block_sm, owner_sm, table, count, drops, members)

    inner = [edge_sm[i].astype(F32) for i in range(4)]
    frac_ref[nx] = halo_above_x[0].astype(F32) * inner[1]
    sides[0:2] = halo_below_y[...].astype(F32) * inner[2]
    sides[2:3] = halo_above_y[...].astype(F32) * inner[3]
    row = lax.broadcasted_iota(jnp.int32, (8, LANES), 0)
    row_last, row_first = row == 7, row == 0
    along = lax.broadcasted_iota(jnp.int32, (nz, nz), 0)
    across = lax.broadcasted_iota(jnp.int32, (nz, nz), 1)
    shift_left = jnp.where(along == across + 1, 1.0, 0.0).astype(BF16)
    difference = jnp.where(
        along == across, 1.0, jnp.where(along + 1 == across, -1.0, 0.0)
    ).astype(BF16)

    def flux(speed, lower, upper):
        return speed * jnp.where(speed > 0, lower, upper)

    frac_in(0).wait()
    flux_low[...] = flux(
        halo_below_x[1].astype(F32) * inner[0], halo_below_x[0].astype(F32), frac_ref[0]
    )

    def look_right(piece, right):
        cells = frac_ref[pl.ds(piece * chunk, chunk)].reshape(chunk * ny, nz).astype(BF16)
        right[...] = jnp.dot(cells, shift_left, preferred_element_type=F32).reshape(
            chunk, ny, nz
        )

    def finish(piece, third, rest):
        change = jnp.dot(
            third[...].reshape(chunk * ny, nz), difference, preferred_element_type=F32
        ).reshape(chunk, ny, nz)
        frac_out[pl.ds(piece * chunk, chunk)] = jnp.minimum(rest[...] - courant * change, 1.0)

    def layer(x, level, right, third, rest):
        side = sides[:, pl.ds(x, 1), :]
        for h in range(nz // LANES):
            lanes = slice(LANES * h, LANES * h + LANES)
            here = frac_ref[x, 0:8, lanes]
            edge = flux(side[1, :, lanes], side[0, :, lanes], here[0:1])
            carried = jnp.broadcast_to(edge, (8, LANES))
            turned_f = pltpu.roll(here, 7, 0)
            for p in range(ny // 16):
                pair = slice(16 * p, 16 * p + 16)
                u = vel_ref[0, x, pair, lanes].astype(F32)
                v = vel_ref[1, x, pair, lanes].astype(F32)
                w = vel_ref[2, x, pair, lanes]
                both = frac_ref[x, pair, lanes]
                third[level, pair, lanes] = flux(
                    w, both.astype(BF16), right[level, pair, lanes].astype(BF16)
                )
                for t in (2 * p, 2 * p + 1):
                    rows = slice(8 * t, 8 * t + 8)
                    half = slice(8 * (t % 2), 8 * (t % 2) + 8)
                    here = both[half]
                    out_x = flux(u[half], here, frac_ref[x + 1, rows, lanes])
                    change = out_x - flux_low[rows, lanes]
                    flux_low[rows, lanes] = out_x
                    if t + 1 < ny // 8:
                        following = frac_ref[x, 8 * t + 8:8 * t + 16, lanes]
                        turned_next = pltpu.roll(following, 7, 0)
                    else:
                        turned_next = jnp.broadcast_to(side[2, :, lanes], (8, LANES))
                    up = jnp.where(row_last, turned_next, turned_f)
                    turned_f = turned_next
                    out_y = flux(v[half], here, up)
                    rolled = pltpu.roll(out_y, 1, 0)
                    change = change + (out_y - jnp.where(row_first, carried, rolled))
                    carried = rolled
                    rest[level, rows, lanes] = here - courant * change

    pieces = depth // chunk
    total = nx // chunk
    look_right(0, right_even)

    def one_step(step, _):
        for copy in vel_in(step):
            copy.wait()

        @pl.when(step + 1 < steps)
        def _():
            frac_in(step + 1).wait()

        first = step * pieces
        even = (right_even, third_even, rest_even)
        odd = (right_odd, third_odd, rest_odd)
        for k in range(pieces):
            now, other = (even, odd) if k % 2 == 0 else (odd, even)
            look_right(jnp.minimum(first + k + 1, total - 1), other[0])
            finish(jnp.maximum(first + k - 1, 0), other[1], other[2])
            for level in range(chunk):
                layer((first + k) * chunk + level, level, *now)

        @pl.when(step > 0)
        def _():
            frac_copy(step - 1).start()

        return 0

    lax.fori_loop(0, steps, one_step, 0)
    finish(total - 1, third_odd, rest_odd)
    frac_copy(steps - 1).start()

    nothing = jnp.where(
        lax.broadcasted_iota(jnp.int32, (4 * EDGE, EDGE * EDGE), 0) >= 3 * EDGE, 1.0, 0.0
    ).astype(BF16)

    def some_windows(first, _):
        for more in range(GROUP * CAP):
            slot = first * GROUP * CAP + more
            x, y, z, shift = corner(jnp.maximum(table[slot], 0), blocks_y, blocks_z)
            spot = (pl.ds(x, EDGE), pl.ds(y, EDGE), pl.ds(z, LANES))
            window = window_of(shift, vel_ref, frac_ref, spot)
            windows_ref[slot] = jnp.where(table[slot] >= 0, window, nothing)
        return 0

    lax.fori_loop(0, members // GROUP, some_windows, 0)

    for step in range(steps):
        frac_copy(step).wait()


def in_hbm(*arrays):
    return [pltpu.with_memory_space_constraint(array, pltpu.HBM) for array in arrays]


def advect(block_ids, owners, edges, volume_frac, velocity, below_x, above_x, below_y, above_y, members):
    nx, ny, nz = volume_frac.shape
    slots = members * CAP
    steps = nx // 8
    chunk = 4
    return pl.pallas_call(
        functools.partial(advect_body, ny // EDGE, nz // EDGE),
        in_specs=[pl.BlockSpec(memory_space=pltpu.HBM)] * 2
        + [pl.BlockSpec(memory_space=pltpu.SMEM)]
        + [pl.BlockSpec(memory_space=pltpu.VMEM)] * 4
        + [pl.BlockSpec(memory_space=pltpu.HBM)] * 2,
        out_specs=[
            pl.BlockSpec(memory_space=pltpu.HBM),
            pl.BlockSpec(memory_space=pltpu.VMEM),
        ],
        out_shape=[
            jax.ShapeDtypeStruct(volume_frac.shape, F32),
            jax.ShapeDtypeStruct((slots, 4 * EDGE, EDGE * EDGE), BF16),
        ],
        scratch_shapes=[
            pltpu.SMEM(block_ids.shape, jnp.int32),
            pltpu.SMEM(owners.shape, jnp.int32),
            pltpu.SMEM((slots,), jnp.int32),
            pltpu.SMEM((members,), jnp.int32),
            pltpu.VMEM((nx + 1, ny, nz), F32),
            pltpu.VMEM(velocity.shape, BF16),
            pltpu.VMEM(volume_frac.shape, F32),
            pltpu.VMEM((3, nx, nz), F32),
            pltpu.VMEM((ny, nz), F32),
            pltpu.VMEM((chunk, ny, nz), F32),
            pltpu.VMEM((chunk, ny, nz), F32),
            pltpu.VMEM((chunk, ny, nz), BF16),
            pltpu.VMEM((chunk, ny, nz), BF16),
            pltpu.VMEM((chunk, ny, nz), F32),
            pltpu.VMEM((chunk, ny, nz), F32),
            pltpu.SemaphoreType.DMA((5, steps)),
            pltpu.SemaphoreType.DMA((2,)),
        ],
        compiler_params=params(),
        cost_estimate=pl.CostEstimate(
            flops=8 * (60 * volume_frac.size + 4 * volume_frac.size * nz),
            bytes_accessed=8 * (2 * volume_frac.size * 4 + velocity.size * 2),
            transcendentals=0,
        ),
        name="advect",
    )(
        *in_hbm(block_ids, owners), edges, below_x, above_x, below_y, above_y,
        *in_hbm(volume_frac, velocity),
    )


def sample_body(parcels_ref, windows_ref, out_ref, kept_ref):
    members = parcels_ref.shape[0]
    parcels = parcels_ref.shape[-1]

    def sample(slot, member, place):
        cell = parcels_ref[member, 5, place:place + 1, :].astype(jnp.int32)
        spread = jnp.dot(windows_ref[slot], rows_of_cell(cell), preferred_element_type=F32)
        mask = lax.broadcasted_iota(jnp.int32, (EDGE, parcels), 0) == jnp.bitwise_and(
            cell, EDGE - 1
        )
        return [
            jnp.sum(
                jnp.where(mask, spread[k * EDGE:(k + 1) * EDGE], 0.0), axis=0, keepdims=True
            )
            for k in range(4)
        ]

    together = 2 * GROUP

    def some_members(first_member, _):
        for more in range(together):
            member = first_member * together + more
            first = sample(member * CAP, member, 0)
            second = sample(member * CAP + 1, member, 1)
            rows = [value for pair in zip(first, second) for value in pair]
            sampled = jnp.concatenate(rows, axis=0).astype(BF16)
            out_ref[member] = sampled
            kept_ref[member] = sampled
        return 0

    lax.fori_loop(0, members // together, some_members, 0)


def sample_parcels(parcels, windows):
    members, _, _, count = parcels.shape
    return pl.pallas_call(
        sample_body,
        in_specs=[pl.BlockSpec(memory_space=pltpu.VMEM)] * 2,
        out_specs=[pl.BlockSpec(memory_space=pltpu.VMEM)] * 2,
        out_shape=[jax.ShapeDtypeStruct((members, 4 * CAP, count), BF16)] * 2,
        compiler_params=params(),
        name="sample",
    )(parcels, windows)


def source_body(
    blocks_y, blocks_z, block_hbm, owner_hbm, parcels_ref, sampled_ref, vel_hbm,
    vel_next,
    block_sm, owner_sm, table, count, order, begins, ends, vel_ref, sems, scalar_sems,
):
    members = parcels_ref.shape[0]
    parcels = parcels_ref.shape[-1]
    slots = members * CAP
    steps = sems.shape[1]
    together = GROUP * CAP
    rounds = slots // together

    def vel_in(step):
        return [
            pltpu.make_async_copy(
                vel_hbm.at[k, pl.ds(step * EDGE, EDGE)], vel_ref.at[k, pl.ds(step * EDGE, EDGE)],
                sems.at[k, step],
            )
            for k in range(3)
        ]

    def vel_copy(step):
        return [
            pltpu.make_async_copy(
                vel_ref.at[k, pl.ds(step * EDGE, EDGE)], vel_next.at[k, pl.ds(step * EDGE, EDGE)],
                sems.at[3 + k, step],
            )
            for k in range(3)
        ]

    scalars = [
        pltpu.make_async_copy(block_hbm, block_sm, scalar_sems.at[0]),
        pltpu.make_async_copy(owner_hbm, owner_sm, scalar_sems.at[1]),
    ]
    for copy in scalars:
        copy.start()
    for step in range(steps):
        for copy in vel_in(step):
            copy.start()
    for copy in scalars:
        copy.wait()
    slot_table(block_sm, owner_sm, table, count, block_sm.shape[0], members)

    filled = 0
    for step in range(steps):
        begins[step] = filled

        def enter(slot, at):
            mine = jnp.maximum(table[slot], 0) // (blocks_y * blocks_z) == step

            @pl.when(mine)
            def _():
                order[at] = slot

            return at + mine.astype(jnp.int32)

        filled = lax.fori_loop(0, slots, enter, filled)
        ends[step] = filled

    def source_of(slot):
        block = table[slot]
        spot = corner(jnp.maximum(block, 0), blocks_y, blocks_z)
        member = slot // CAP
        odd = slot % CAP == 1
        both = [parcels_ref[member, k] for k in range(FIELDS)]
        field = [jnp.where(odd, value[1:2], value[0:1]) for value in both]
        got = sampled_ref[member].astype(F32)
        value = [
            jnp.where(odd, got[CAP * k + 1:CAP * k + 2], got[CAP * k:CAP * k + 1])
            for k in range(4)
        ]
        cell = field[5].astype(jnp.int32)
        factor = field[3] * (1.0 - value[3])
        wanted = jnp.where(block >= 0, jnp.bitwise_and(cell, EDGE - 1), -1)
        third = lax.broadcasted_iota(jnp.int32, (EDGE, parcels), 0).astype(F32).astype(BF16)
        hits = third == wanted.astype(F32).astype(BF16)
        deposits = jnp.concatenate(
            [
                jnp.where(
                    hits,
                    (field[4] * (factor * (value[k] - field[k]))).astype(BF16),
                    jnp.zeros((1, parcels), BF16),
                )
                for k in range(3)
            ],
            axis=0,
        )
        source = lax.dot_general(
            rows_of_cell(cell), deposits, (((1,), (1,)), ((), ())), preferred_element_type=F32
        )
        wide = jnp.concatenate([source, jnp.zeros((EDGE * EDGE, LANES - 3 * EDGE), F32)], axis=1)
        at = lax.broadcasted_iota(jnp.int32, (EDGE * EDGE, LANES), 1) - spot[3]
        inside = (at >= 0) & (at < EDGE)
        placed = [
            jnp.where(inside, pltpu.roll(wide, lax.rem(spot[3] + LANES - k * EDGE, LANES), 1), 0.0)
            for k in range(3)
        ]
        return spot, [piece.astype(BF16) for piece in placed]

    def add_source(spot, source):
        x, y, z, _ = spot
        for k in range(3):
            here = (k, pl.ds(x, EDGE), pl.ds(y, EDGE), pl.ds(z, LANES))
            vel_ref[here] = vel_ref[here] + source[k].reshape(EDGE, EDGE, LANES)

    def one_round(turn, _):
        found = [source_of(order[turn * together + more]) for more in range(together)]
        first, last = [], []
        for step in range(steps):
            first.append(jnp.minimum(begins[step] // together, rounds - 1))
            last.append(jnp.maximum(first[step], (ends[step] + together - 1) // together - 1))
        for step in range(steps):

            @pl.when(first[step] == turn)
            def _():
                for copy in vel_in(step):
                    copy.wait()

        for spot, source in found:
            add_source(spot, source)
        for step in range(steps):

            @pl.when(last[step] == turn)
            def _():
                for copy in vel_copy(step):
                    copy.start()

        return 0

    lax.fori_loop(0, rounds, one_round, 0)
    for step in range(steps):
        for copy in vel_copy(step):
            copy.wait()


def add_drag(block_ids, owners, parcels, sampled, velocity):
    _, nx, ny, nz = velocity.shape
    members = parcels.shape[0]
    slots = members * CAP
    steps = nx // EDGE
    hbm, vmem = pl.BlockSpec(memory_space=pltpu.HBM), pl.BlockSpec(memory_space=pltpu.VMEM)
    return pl.pallas_call(
        functools.partial(source_body, ny // EDGE, nz // EDGE),
        in_specs=[hbm, hbm, vmem, vmem, hbm],
        out_specs=hbm,
        out_shape=jax.ShapeDtypeStruct(velocity.shape, BF16),
        scratch_shapes=[
            pltpu.SMEM(block_ids.shape, jnp.int32),
            pltpu.SMEM(owners.shape, jnp.int32),
            pltpu.SMEM((slots,), jnp.int32),
            pltpu.SMEM((members,), jnp.int32),
            pltpu.SMEM((slots,), jnp.int32),
            pltpu.SMEM((steps,), jnp.int32),
            pltpu.SMEM((steps,), jnp.int32),
            pltpu.VMEM(velocity.shape, BF16),
            pltpu.SemaphoreType.DMA((6, steps)),
            pltpu.SemaphoreType.DMA((2,)),
        ],
        compiler_params=params(),
        name="add_drag",
    )(*in_hbm(block_ids, owners), parcels, sampled, *in_hbm(velocity))


def drag_body(vel_ref, rate_ref, sampled_ref, out_ref):
    members = vel_ref.shape[0]
    for member in range(members):
        got = sampled_ref[member].astype(F32)
        factor = rate_ref[member] * (1.0 - got[3 * CAP:4 * CAP])
        for k in range(3):
            old = vel_ref[member, k]
            out_ref[member, k] = old + factor * (got[k * CAP:(k + 1) * CAP] - old)


def drag(vel, rate, sampled):
    return pl.pallas_call(
        drag_body,
        out_shape=jax.ShapeDtypeStruct(vel.shape, F32),
        compiler_params=params(),
        name="drag",
    )(vel, rate, sampled)


def per_device(
    volume_frac,
    velocity,
    drop_block,
    drop_owner,
    parcel_vel,
    parcel_rate,
    parcel_weight,
    parcel_cell,
):
    block_ids = drop_block.reshape(-1)
    owners = drop_owner.reshape(-1)
    vel = jnp.swapaxes(parcel_vel[0, 0], 1, 2)
    rate = parcel_rate[0, 0]
    parcels, up_x, down_x, up_y, down_y = pack(
        volume_frac, velocity, vel, rate, parcel_weight[0, 0], parcel_cell[0, 0]
    )
    below_x = passed_around(up_x, "group", 1)
    above_x = passed_around(down_x, "group", -1)
    below_y = passed_around(up_y, "member", 1)
    above_y = passed_around(down_y, "member", -1)
    parcels_in = lax.all_to_all(parcels, "member", split_axis=0, concat_axis=0, tiled=True)
    edges = jnp.stack(
        [
            lax.axis_index("group") > 0,
            lax.axis_index("group") < lax.axis_size("group") - 1,
            lax.axis_index("member") > 0,
            lax.axis_index("member") < lax.axis_size("member") - 1,
        ]
    ).astype(jnp.int32)
    frac_next, windows = advect(
        block_ids, owners, edges, volume_frac, velocity,
        below_x, above_x, below_y, above_y, rate.shape[0],
    )
    parcels_in, windows = lax.optimization_barrier((parcels_in, windows))
    sampled, kept = sample_parcels(parcels_in, windows)
    returned = lax.all_to_all(sampled, "member", split_axis=0, concat_axis=0, tiled=True)
    velocity_next = add_drag(block_ids, owners, parcels_in, kept, velocity)
    vel_next = drag(vel, rate, returned)
    parcel_next = jnp.swapaxes(vel_next, 1, 2)[None, None]
    return (frac_next, velocity_next, parcel_next)


def solution(mesh):
    in_specs = (
        P("group", "member", None),
        P(None, "group", "member", None),
        P("group", "member", None),
        P("group", "member", None, None),
        P("group", "member", None, None, None, None),
        P("group", "member", None, None, None),
        P("group", "member", None, None, None),
        P("group", "member", None, None, None),
    )
    out_specs = (
        P("group", "member", None),
        P(None, "group", "member", None),
        P("group", "member", None, None, None, None),
    )
    return jax.shard_map(
        per_device, mesh=mesh, in_specs=in_specs, out_specs=out_specs, check_vma=False
    )
```

```python
import functools

import jax
import jax.numpy as jnp
from jax import lax
from jax.experimental import pallas as pl
from jax.experimental.pallas import tpu as pltpu
from jax.sharding import PartitionSpec as P

CAP = 2
EDGE = 16
LANES = 128
FIELDS = 6
GROUP = 2

courant = 0.025

F32 = jnp.float32
BF16 = jnp.bfloat16


def passed_around(block, axis, distance):
    size = lax.axis_size(axis)
    return lax.ppermute(block, axis, [(i, (i + distance) % size) for i in range(size)])


def whole(shape):
    return pl.BlockSpec(shape, lambda *_: (0,) * len(shape))


def params(**more):
    return pltpu.CompilerParams(vmem_limit_bytes=24 * 1024 * 1024, **more)


def pack_body(
    vel_hbm, rate_hbm, weight_hbm, cell_hbm, frac_hbm, velocity_hbm,
    parcels_hbm, up_x, down_x, up_y, down_y,
    cells, staged, f_first_x, f_last_x, u_last_x, f_first_y, f_last_y, u_last_y, sems,
):
    nx, ny, nz = frac_hbm.shape
    cells_in = pltpu.make_async_copy(cell_hbm, cells, sems.at[0])
    straight = [
        pltpu.make_async_copy(vel_hbm, staged.at[:, 0:3], sems.at[1]),
        pltpu.make_async_copy(rate_hbm, staged.at[:, 3], sems.at[2]),
        pltpu.make_async_copy(weight_hbm, staged.at[:, 4], sems.at[3]),
    ]
    staged_out = pltpu.make_async_copy(staged, parcels_hbm, sems.at[4])
    pieces = [
        pltpu.make_async_copy(source, piece, sems.at[5 + i])
        for i, (source, piece) in enumerate(
            [
                (frac_hbm.at[:, pl.ds(0, 8)], f_first_y),
                (frac_hbm.at[:, pl.ds(ny - 8, 8)], f_last_y),
                (velocity_hbm.at[1, :, pl.ds(ny - 16, 16)], u_last_y),
                (frac_hbm.at[0], f_first_x),
                (frac_hbm.at[nx - 1], f_last_x),
                (velocity_hbm.at[0, nx - 1], u_last_x),
            ]
        )
    ]
    cells_in.start()
    for copy in straight + pieces:
        copy.start()
    cells_in.wait()
    staged[:, 5] = cells[...].astype(F32)
    for copy in straight:
        copy.wait()
    staged_out.start()
    for copy in pieces:
        copy.wait()
    up_x[0] = f_last_x[...].astype(BF16)
    up_x[1] = u_last_x[...]
    down_x[0] = f_first_x[...].astype(BF16)
    up_y[0] = f_last_y[:, 7, :].astype(BF16)
    up_y[1] = u_last_y[...].astype(F32)[:, 15, :].astype(BF16)
    down_y[0] = f_first_y[:, 0, :].astype(BF16)
    staged_out.wait()


def pack(volume_frac, velocity, vel, rate, weight, cell):
    nx, ny, nz = volume_frac.shape
    members, _, parcels = rate.shape
    return pl.pallas_call(
        pack_body,
        in_specs=[pl.BlockSpec(memory_space=pltpu.HBM)] * 6,
        out_specs=[pl.BlockSpec(memory_space=pltpu.HBM)]
        + [pl.BlockSpec(memory_space=pltpu.VMEM)] * 4,
        out_shape=[
            jax.ShapeDtypeStruct((members, FIELDS, CAP, parcels), F32),
            jax.ShapeDtypeStruct((2, ny, nz), BF16),
            jax.ShapeDtypeStruct((1, ny, nz), BF16),
            jax.ShapeDtypeStruct((2, nx, nz), BF16),
            jax.ShapeDtypeStruct((1, nx, nz), BF16),
        ],
        scratch_shapes=[
            pltpu.VMEM(cell.shape, jnp.int32),
            pltpu.VMEM((members, FIELDS, CAP, parcels), F32),
            pltpu.VMEM((ny, nz), F32),
            pltpu.VMEM((ny, nz), F32),
            pltpu.VMEM((ny, nz), BF16),
            pltpu.VMEM((nx, 8, nz), F32),
            pltpu.VMEM((nx, 8, nz), F32),
            pltpu.VMEM((nx, 16, nz), BF16),
            pltpu.SemaphoreType.DMA((11,)),
        ],
        compiler_params=params(),
        name="pack",
    )(*in_hbm(vel, rate, weight, cell, volume_frac, velocity))


def slot_table(block_sm, owner_sm, table):
    for slot in range(table.shape[0]):
        table[slot] = -1
    owners = []
    for j in range(block_sm.shape[0]):
        owner = owner_sm[j]
        place = 0
        for earlier in owners:
            place = place + (earlier == owner).astype(jnp.int32)
        owners.append(owner)
        table[owner * CAP + place] = block_sm[j]


def slots_by_slab(table, order, steps, blocks_in_slab):
    slabs = [
        parted(jnp.maximum(table[slot], 0), blocks_in_slab)[0] for slot in range(order.shape[0])
    ]
    begins, ends = [], []
    at = 0
    for step in range(steps):
        begins.append(at)
        for slab in slabs:
            at = at + (slab == step).astype(jnp.int32)
        ends.append(at)
    following = list(begins)
    for slot, slab in enumerate(slabs):
        spot = following[0]
        for step in range(1, steps):
            spot = jnp.where(slab == step, following[step], spot)
        order[spot] = slot
        for step in range(steps):
            following[step] = following[step] + (slab == step).astype(jnp.int32)
    return begins, ends


def parted(number, size):
    if size & (size - 1) == 0:
        return lax.shift_right_logical(number, size.bit_length() - 1), jnp.bitwise_and(number, size - 1)
    return number // size, number % size


def corner(block, blocks_y, blocks_z):
    upper, bz = parted(block, blocks_z)
    bx, by = parted(upper, blocks_y)
    tile, place = parted(bz, LANES // EDGE)
    x = bx * EDGE
    return x, pl.multiple_of(by * EDGE, EDGE), pl.multiple_of(tile * LANES, LANES), place * EDGE


def rows_of_cell(cell):
    high = lax.shift_right_logical(cell, 4).astype(F32).astype(BF16)
    rows = lax.broadcasted_iota(jnp.int32, (EDGE * EDGE, cell.shape[-1]), 0)
    hits = rows.astype(F32).astype(BF16) == high
    return jnp.where(hits, jnp.ones_like(high), jnp.zeros_like(high))


def window_of(shift, velocity_ref, frac_ref, spot):
    tile = jnp.concatenate(
        [velocity_ref[(k,) + spot].reshape(EDGE * EDGE, LANES) for k in range(3)]
        + [frac_ref[spot].reshape(EDGE * EDGE, LANES).astype(BF16)],
        axis=1,
    )
    row = lax.broadcasted_iota(jnp.int32, (4 * EDGE, 4 * LANES), 0)
    column = lax.broadcasted_iota(jnp.int32, (4 * EDGE, 4 * LANES), 1)
    wanted = row // EDGE * LANES + row % EDGE + shift
    picker = jnp.where(column == wanted, 1.0, 0.0).astype(BF16)
    return lax.dot_general(
        picker, tile, (((1,), (1,)), ((), ())), preferred_element_type=F32
    ).astype(BF16)


def advect_body(
    blocks_y, blocks_z,
    block_hbm, owner_hbm,
    halo_below_x, halo_above_x, halo_below_y, halo_above_y, frac_hbm, vel_hbm,
    frac_next, windows_ref,
    block_sm, owner_sm, table, frac_ref, vel_ref, frac_out, sides, flux_low,
    right_even, right_odd, third_even, third_odd, rest_even, rest_odd, sems, scalar_sems,
):
    nx, ny, nz = frac_out.shape
    steps = sems.shape[1]
    depth = nx // steps
    chunk = right_even.shape[0]

    def part(step):
        return pl.ds(step * depth, depth)

    def frac_in(step):
        return pltpu.make_async_copy(
            frac_hbm.at[part(step)], frac_ref.at[part(step)], sems.at[0, step]
        )

    def vel_in(step):
        return [
            pltpu.make_async_copy(
                vel_hbm.at[k, part(step)], vel_ref.at[k, part(step)], sems.at[2 + k, step]
            )
            for k in range(3)
        ]

    def frac_copy(step):
        return pltpu.make_async_copy(
            frac_out.at[part(step)], frac_next.at[part(step)], sems.at[1, step]
        )

    scalars = [
        pltpu.make_async_copy(block_hbm, block_sm, scalar_sems.at[0]),
        pltpu.make_async_copy(owner_hbm, owner_sm, scalar_sems.at[1]),
    ]
    for copy in scalars:
        copy.start()
    frac_in(0).start()
    for step in range(steps):
        for copy in vel_in(step):
            copy.start()
        if step + 1 < steps:
            frac_in(step + 1).start()


    inner = []
    for axis in ("group", "member"):
        at, size = lax.axis_index(axis), lax.axis_size(axis)
        inner += [(at > 0).astype(F32), (at < size - 1).astype(F32)]
    frac_ref[nx] = halo_above_x[0].astype(F32) * inner[1]
    sides[0:2] = halo_below_y[...].astype(F32) * inner[2]
    sides[2:3] = halo_above_y[...].astype(F32) * inner[3]
    row = lax.broadcasted_iota(jnp.int32, (8, LANES), 0)
    row_last, row_first = row == 7, row == 0
    along = lax.broadcasted_iota(jnp.int32, (nz, nz), 0)
    across = lax.broadcasted_iota(jnp.int32, (nz, nz), 1)
    shift_left = jnp.where(along == across + 1, 1.0, 0.0).astype(BF16)
    difference = jnp.where(
        along == across, 1.0, jnp.where(along + 1 == across, -1.0, 0.0)
    ).astype(BF16)

    def flux(speed, lower, upper):
        return speed * jnp.where(speed > 0, lower, upper)

    frac_in(0).wait()
    flux_low[...] = flux(
        halo_below_x[1].astype(F32) * inner[0], halo_below_x[0].astype(F32), frac_ref[0]
    )

    def look_right(piece, right):
        cells = frac_ref[pl.ds(piece * chunk, chunk)].reshape(chunk * ny, nz).astype(BF16)
        right[...] = jnp.dot(cells, shift_left, preferred_element_type=F32).reshape(
            chunk, ny, nz
        )

    def finish(piece, third, rest):
        change = jnp.dot(
            third[...].reshape(chunk * ny, nz), difference, preferred_element_type=F32
        ).reshape(chunk, ny, nz)
        frac_out[pl.ds(piece * chunk, chunk)] = jnp.minimum(rest[...] - courant * change, 1.0)

    def layer(x, level, right, third, rest):
        side = sides[:, pl.ds(x, 1), :]
        for h in range(nz // LANES):
            lanes = slice(LANES * h, LANES * h + LANES)
            here = frac_ref[x, 0:8, lanes]
            edge = flux(side[1, :, lanes], side[0, :, lanes], here[0:1])
            carried = jnp.broadcast_to(edge, (8, LANES))
            turned_f = pltpu.roll(here, 7, 0)
            for p in range(ny // 16):
                pair = slice(16 * p, 16 * p + 16)
                u = vel_ref[0, x, pair, lanes].astype(F32)
                v = vel_ref[1, x, pair, lanes].astype(F32)
                w = vel_ref[2, x, pair, lanes]
                both = frac_ref[x, pair, lanes]
                third[level, pair, lanes] = flux(
                    w, both.astype(BF16), right[level, pair, lanes].astype(BF16)
                )
                for t in (2 * p, 2 * p + 1):
                    rows = slice(8 * t, 8 * t + 8)
                    half = slice(8 * (t % 2), 8 * (t % 2) + 8)
                    here = both[half]
                    out_x = flux(u[half], here, frac_ref[x + 1, rows, lanes])
                    change = out_x - flux_low[rows, lanes]
                    flux_low[rows, lanes] = out_x
                    if t + 1 < ny // 8:
                        following = frac_ref[x, 8 * t + 8:8 * t + 16, lanes]
                        turned_next = pltpu.roll(following, 7, 0)
                    else:
                        turned_next = jnp.broadcast_to(side[2, :, lanes], (8, LANES))
                    up = jnp.where(row_last, turned_next, turned_f)
                    turned_f = turned_next
                    out_y = flux(v[half], here, up)
                    rolled = pltpu.roll(out_y, 1, 0)
                    change = change + (out_y - jnp.where(row_first, carried, rolled))
                    carried = rolled
                    rest[level, rows, lanes] = here - courant * change

    pieces = depth // chunk
    total = nx // chunk
    look_right(0, right_even)

    nothing = jnp.where(
        lax.broadcasted_iota(jnp.int32, (4 * EDGE, EDGE * EDGE), 0) >= 3 * EDGE, 1.0, 0.0
    ).astype(BF16)
    together = GROUP * CAP

    def some_windows(turn, _):
        for more in range(together):
            slot = turn * together + more
            x, y, z, shift = corner(jnp.maximum(table[slot], 0), blocks_y, blocks_z)
            spot = (pl.ds(x, EDGE), pl.ds(y, EDGE), pl.ds(z, LANES))
            window = window_of(shift, vel_ref, frac_ref, spot)
            windows_ref[slot] = jnp.where(table[slot] >= 0, window, nothing)
        return 0

    def one_step(step, _):
        @pl.when(step == 1)
        def _():
            for copy in scalars:
                copy.wait()
            slot_table(block_sm, owner_sm, table)

        for copy in vel_in(step):
            copy.wait()

        @pl.when(step + 1 < steps)
        def _():
            frac_in(step + 1).wait()

        first = step * pieces
        even = (right_even, third_even, rest_even)
        odd = (right_odd, third_odd, rest_odd)
        for k in range(pieces):
            now, other = (even, odd) if k % 2 == 0 else (odd, even)
            look_right(jnp.minimum(first + k + 1, total - 1), other[0])
            finish(jnp.maximum(first + k - 1, 0), other[1], other[2])
            for level in range(chunk):
                layer((first + k) * chunk + level, level, *now)

        @pl.when(step > 0)
        def _():
            frac_copy(step - 1).start()

        return 0

    lax.fori_loop(0, steps, one_step, 0)
    finish(total - 1, third_odd, rest_odd)
    frac_copy(steps - 1).start()
    for turn in range(table.shape[0] // together):
        some_windows(turn, 0)

    for step in range(steps):
        frac_copy(step).wait()


def in_hbm(*arrays):
    return [pltpu.with_memory_space_constraint(array, pltpu.HBM) for array in arrays]


def advect(block_ids, owners, volume_frac, velocity, below_x, above_x, below_y, above_y, members):
    nx, ny, nz = volume_frac.shape
    slots = members * CAP
    steps = nx // 8
    chunk = 4
    return pl.pallas_call(
        functools.partial(advect_body, ny // EDGE, nz // EDGE),
        in_specs=[pl.BlockSpec(memory_space=pltpu.HBM)] * 2
        + [pl.BlockSpec(memory_space=pltpu.VMEM)] * 4
        + [pl.BlockSpec(memory_space=pltpu.HBM)] * 2,
        out_specs=[
            pl.BlockSpec(memory_space=pltpu.HBM),
            pl.BlockSpec(memory_space=pltpu.VMEM),
        ],
        out_shape=[
            jax.ShapeDtypeStruct(volume_frac.shape, F32),
            jax.ShapeDtypeStruct((slots, 4 * EDGE, EDGE * EDGE), BF16),
        ],
        scratch_shapes=[
            pltpu.SMEM(block_ids.shape, jnp.int32),
            pltpu.SMEM(owners.shape, jnp.int32),
            pltpu.SMEM((slots,), jnp.int32),
            pltpu.VMEM((nx + 1, ny, nz), F32),
            pltpu.VMEM(velocity.shape, BF16),
            pltpu.VMEM(volume_frac.shape, F32),
            pltpu.VMEM((3, nx, nz), F32),
            pltpu.VMEM((ny, nz), F32),
            pltpu.VMEM((chunk, ny, nz), F32),
            pltpu.VMEM((chunk, ny, nz), F32),
            pltpu.VMEM((chunk, ny, nz), BF16),
            pltpu.VMEM((chunk, ny, nz), BF16),
            pltpu.VMEM((chunk, ny, nz), F32),
            pltpu.VMEM((chunk, ny, nz), F32),
            pltpu.SemaphoreType.DMA((5, steps)),
            pltpu.SemaphoreType.DMA((2,)),
        ],
        compiler_params=params(),
        cost_estimate=pl.CostEstimate(
            flops=8 * (60 * volume_frac.size + 4 * volume_frac.size * nz),
            bytes_accessed=8 * (2 * volume_frac.size * 4 + velocity.size * 2),
            transcendentals=0,
        ),
        name="advect",
    )(
        *in_hbm(block_ids, owners), below_x, above_x, below_y, above_y,
        *in_hbm(volume_frac, velocity),
    )


def sample_body(parcels_ref, windows_ref, out_ref, kept_ref):
    members = parcels_ref.shape[0]
    parcels = parcels_ref.shape[-1]

    def sample(slot, member, place):
        cell = parcels_ref[member, 5, place:place + 1, :].astype(jnp.int32)
        spread = jnp.dot(windows_ref[slot], rows_of_cell(cell), preferred_element_type=F32)
        mask = lax.broadcasted_iota(jnp.int32, (EDGE, parcels), 0) == jnp.bitwise_and(
            cell, EDGE - 1
        )
        return [
            jnp.sum(
                jnp.where(mask, spread[k * EDGE:(k + 1) * EDGE], 0.0), axis=0, keepdims=True
            )
            for k in range(4)
        ]

    together = 2 * GROUP

    def some_members(first_member, _):
        for more in range(together):
            member = first_member * together + more
            first = sample(member * CAP, member, 0)
            second = sample(member * CAP + 1, member, 1)
            rows = [value for pair in zip(first, second) for value in pair]
            sampled = jnp.concatenate(rows, axis=0).astype(BF16)
            out_ref[member] = sampled
            kept_ref[member] = sampled
        return 0

    lax.fori_loop(0, members // together, some_members, 0)


def sample_parcels(parcels, windows):
    members, _, _, count = parcels.shape
    return pl.pallas_call(
        sample_body,
        in_specs=[pl.BlockSpec(memory_space=pltpu.VMEM)] * 2,
        out_specs=[pl.BlockSpec(memory_space=pltpu.VMEM)] * 2,
        out_shape=[jax.ShapeDtypeStruct((members, 4 * CAP, count), BF16)] * 2,
        compiler_params=params(),
        name="sample",
    )(parcels, windows)


def source_body(
    blocks_y, blocks_z, block_hbm, owner_hbm, parcels_ref, sampled_ref, vel_hbm,
    vel_next,
    block_sm, owner_sm, table, order, vel_ref, sems, scalar_sems,
):
    members = parcels_ref.shape[0]
    parcels = parcels_ref.shape[-1]
    slots = members * CAP
    steps = sems.shape[1]
    together = GROUP * CAP
    rounds = slots // together

    def vel_in(step):
        return [
            pltpu.make_async_copy(
                vel_hbm.at[k, pl.ds(step * EDGE, EDGE)], vel_ref.at[k, pl.ds(step * EDGE, EDGE)],
                sems.at[k, step],
            )
            for k in range(3)
        ]

    def vel_copy(step):
        return [
            pltpu.make_async_copy(
                vel_ref.at[k, pl.ds(step * EDGE, EDGE)], vel_next.at[k, pl.ds(step * EDGE, EDGE)],
                sems.at[3 + k, step],
            )
            for k in range(3)
        ]

    scalars = [
        pltpu.make_async_copy(block_hbm, block_sm, scalar_sems.at[0]),
        pltpu.make_async_copy(owner_hbm, owner_sm, scalar_sems.at[1]),
    ]
    for copy in scalars:
        copy.start()
    for step in range(steps):
        for copy in vel_in(step):
            copy.start()
    for copy in scalars:
        copy.wait()
    slot_table(block_sm, owner_sm, table)
    begins, ends = slots_by_slab(table, order, steps, blocks_y * blocks_z)

    def source_of(slot):
        block = table[slot]
        spot = corner(jnp.maximum(block, 0), blocks_y, blocks_z)
        member, place = parted(slot, CAP)
        odd = place == 1
        both = [parcels_ref[member, k] for k in range(FIELDS)]
        field = [jnp.where(odd, value[1:2], value[0:1]) for value in both]
        got = sampled_ref[member].astype(F32)
        value = [
            jnp.where(odd, got[CAP * k + 1:CAP * k + 2], got[CAP * k:CAP * k + 1])
            for k in range(4)
        ]
        cell = field[5].astype(jnp.int32)
        factor = field[3] * (1.0 - value[3])
        wanted = jnp.where(block >= 0, jnp.bitwise_and(cell, EDGE - 1), -1)
        third = lax.broadcasted_iota(jnp.int32, (EDGE, parcels), 0).astype(F32).astype(BF16)
        hits = third == wanted.astype(F32).astype(BF16)
        deposits = jnp.concatenate(
            [
                jnp.where(
                    hits,
                    (field[4] * (factor * (value[k] - field[k]))).astype(BF16),
                    jnp.zeros((1, parcels), BF16),
                )
                for k in range(3)
            ],
            axis=0,
        )
        source = lax.dot_general(
            rows_of_cell(cell), deposits, (((1,), (1,)), ((), ())), preferred_element_type=F32
        )
        wide = jnp.concatenate([source, jnp.zeros((EDGE * EDGE, LANES - 3 * EDGE), F32)], axis=1)
        at = lax.broadcasted_iota(jnp.int32, (EDGE * EDGE, LANES), 1) - spot[3]
        inside = (at >= 0) & (at < EDGE)
        placed = [
            jnp.where(inside, pltpu.roll(wide, lax.rem(spot[3] + LANES - k * EDGE, LANES), 1), 0.0)
            for k in range(3)
        ]
        return spot, [piece.astype(BF16) for piece in placed]

    def add_source(spot, source):
        x, y, z, _ = spot
        for k in range(3):
            here = (k, pl.ds(x, EDGE), pl.ds(y, EDGE), pl.ds(z, LANES))
            vel_ref[here] = vel_ref[here] + source[k].reshape(EDGE, EDGE, LANES)

    first, last = [], []
    for step in range(steps):
        first.append(jnp.minimum(parted(begins[step], together)[0], rounds - 1))
        last.append(
            jnp.maximum(first[step], parted(ends[step] + together - 1, together)[0] - 1)
        )

    def sources_of(turn):
        return [source_of(order[turn * together + more]) for more in range(together)]

    found = sources_of(0)
    for turn in range(rounds):
        for step in range(steps):

            @pl.when(first[step] == turn)
            def _():
                for copy in vel_in(step):
                    copy.wait()

        following = sources_of(turn + 1) if turn + 1 < rounds else None
        for spot, source in found:
            add_source(spot, source)
        found = following
        for step in range(steps):

            @pl.when(last[step] == turn)
            def _():
                for copy in vel_copy(step):
                    copy.start()

    for step in range(steps):
        for copy in vel_copy(step):
            copy.wait()


def add_drag(block_ids, owners, parcels, sampled, velocity):
    _, nx, ny, nz = velocity.shape
    members = parcels.shape[0]
    slots = members * CAP
    steps = nx // EDGE
    hbm, vmem = pl.BlockSpec(memory_space=pltpu.HBM), pl.BlockSpec(memory_space=pltpu.VMEM)
    return pl.pallas_call(
        functools.partial(source_body, ny // EDGE, nz // EDGE),
        in_specs=[hbm, hbm, vmem, vmem, hbm],
        out_specs=hbm,
        out_shape=jax.ShapeDtypeStruct(velocity.shape, BF16),
        scratch_shapes=[
            pltpu.SMEM(block_ids.shape, jnp.int32),
            pltpu.SMEM(owners.shape, jnp.int32),
            pltpu.SMEM((slots,), jnp.int32),
            pltpu.SMEM((slots,), jnp.int32),
            pltpu.VMEM(velocity.shape, BF16),
            pltpu.SemaphoreType.DMA((6, steps)),
            pltpu.SemaphoreType.DMA((2,)),
        ],
        compiler_params=params(),
        name="add_drag",
    )(*in_hbm(block_ids, owners), parcels, sampled, *in_hbm(velocity))


def drag_body(vel_ref, rate_ref, sampled_ref, out_ref):
    members = vel_ref.shape[0]
    for member in range(members):
        got = sampled_ref[member].astype(F32)
        factor = rate_ref[member] * (1.0 - got[3 * CAP:4 * CAP])
        for k in range(3):
            old = vel_ref[member, k]
            out_ref[member, k] = old + factor * (got[k * CAP:(k + 1) * CAP] - old)


def drag(vel, rate, sampled):
    return pl.pallas_call(
        drag_body,
        out_shape=jax.ShapeDtypeStruct(vel.shape, F32),
        compiler_params=params(),
        name="drag",
    )(vel, rate, sampled)


def per_device(
    volume_frac,
    velocity,
    drop_block,
    drop_owner,
    parcel_vel,
    parcel_rate,
    parcel_weight,
    parcel_cell,
):
    block_ids = drop_block.reshape(-1)
    owners = drop_owner.reshape(-1)
    vel = jnp.swapaxes(parcel_vel[0, 0], 1, 2)
    rate = parcel_rate[0, 0]
    parcels, up_x, down_x, up_y, down_y = pack(
        volume_frac, velocity, vel, rate, parcel_weight[0, 0], parcel_cell[0, 0]
    )
    below_x = passed_around(up_x, "group", 1)
    above_x = passed_around(down_x, "group", -1)
    below_y = passed_around(up_y, "member", 1)
    above_y = passed_around(down_y, "member", -1)
    parcels_in = lax.all_to_all(parcels, "member", split_axis=0, concat_axis=0, tiled=True)
    frac_next, windows = advect(
        block_ids, owners, volume_frac, velocity,
        below_x, above_x, below_y, above_y, rate.shape[0],
    )
    parcels_in, windows = lax.optimization_barrier((parcels_in, windows))
    sampled, kept = sample_parcels(parcels_in, windows)
    returned = lax.all_to_all(sampled, "member", split_axis=0, concat_axis=0, tiled=True)
    velocity_next = add_drag(block_ids, owners, parcels_in, kept, velocity)
    vel_next = drag(vel, rate, returned)
    parcel_next = jnp.swapaxes(vel_next, 1, 2)[None, None]
    return (frac_next, velocity_next, parcel_next)


def solution(mesh):
    in_specs = (
        P("group", "member", None),
        P(None, "group", "member", None),
        P("group", "member", None),
        P("group", "member", None, None),
        P("group", "member", None, None, None, None),
        P("group", "member", None, None, None),
        P("group", "member", None, None, None),
        P("group", "member", None, None, None),
    )
    out_specs = (
        P("group", "member", None),
        P(None, "group", "member", None),
        P("group", "member", None, None, None, None),
    )
    return jax.shard_map(
        per_device, mesh=mesh, in_specs=in_specs, out_specs=out_specs, check_vma=False
    )
```
